32 devices in a mesh: seq: 8 (over z, y), tp: 4 (over x, core).
Axes of the slice: x: 2, y: 2, z: 4, core: 2. Of those that a mesh axis runs over, the one named last changes fastest.
Arguments:
- att_query: bfloat16 [1024, 8192], P('seq', 'tp'), may hold values from -12 to 12
- att_key: bfloat16 [1024, 8192], P('seq', 'tp'), may hold values from -6 to 6
- att_value: bfloat16 [1024, 8192], P('seq', 'tp'), may hold values from -6 to 6
- past_key: bfloat16 [256, 8192], P(('seq', 'tp')), may hold values from -6 to 6
- past_value: bfloat16 [256, 8192], P(('seq', 'tp')), may hold values from -6 to 6
Outputs:
- attn_out: bfloat16 [1024, 8192], P('seq', 'tp')
The draws below stay inside these ranges and needn't reach their ends.
All inputs are finite; a program needn't handle non-finite values.
Results may differ from the reference program's by a relative error of at most 0.006.
Values may be sent and summed in bfloat16 or wider, within the bound.
A program may use at most 128 MiB of HBM per device.

```python
import jax
import jax.numpy as jnp
from jax import lax

D = 8192
HEAD = 128
HEADS = 64
STRETCH = 1024
HIST = 256


def draw_att_query(key, part):
    source = jax.random.fold_in(key, 11)
    drawn = jnp.clip(2.5 * jax.random.normal(source, (STRETCH, D), jnp.float32), -12.0, 12.0)
    return drawn.astype(jnp.bfloat16)


def draw_past_key(key, part):
    source = jax.random.fold_in(key, 21)
    drawn = jnp.clip(jax.random.normal(source, (HIST, D), jnp.float32), -6.0, 6.0)
    return drawn.astype(jnp.bfloat16)


def steps_of(rng, dims, cuts, least, top_value):
    factor_of = 1.0
    for axis_at, shards_of in cuts:
        heights = jax.random.uniform(jax.random.fold_in(jax.random.fold_in(rng, 6), axis_at), (shards_of,), jnp.float32, least / len(cuts), top_value / len(cuts))
        factor_of = factor_of * jnp.repeat(jnp.exp(heights), dims[axis_at] // shards_of).reshape((-1,) + (1,) * (len(dims) - 1 - axis_at))
    return factor_of


def bell_draw(stream_key, dims, width, limit, cuts=(), held_as=jnp.bfloat16):
    array = jax.random.normal(stream_key, dims, jnp.float32) * width
    if len(cuts) > 0:
        array = steps_of(stream_key, dims, cuts, -0.22, 0.18) * array
    return jnp.clip(array, min=-limit, max=limit).astype(held_as)


def setup_inputs(seed: int = 0) -> dict:
    key_of = jax.random.split(jax.random.key(seed), 6)
    att_query = draw_att_query(jax.random.fold_in(key_of[5], 71), 0)
    att_key = bell_draw(key_of[1], (STRETCH, D), 1.0, 6.0, ((0, 8), (1, 4)))
    att_value = bell_draw(key_of[2], (STRETCH, D), 1.0, 6.0, ((0, 8), (1, 4)))
    past_key = draw_past_key(jax.random.fold_in(key_of[5], 71), 0)
    past_value = bell_draw(key_of[4], (HIST, D), 1.0, 6.0, ((0, 32),))
    return dict(att_query=att_query, att_key=att_key, att_value=att_value, past_key=past_key, past_value=past_value)


NEGATIVE = -1e30


def reference(att_query, att_key, att_value, past_key, past_value):
    keys = jnp.concatenate([past_key, att_key], 0)
    values = jnp.concatenate([past_value, att_value], 0)
    query_pos = HIST + jnp.arange(STRETCH, dtype=jnp.int32)
    key_pos = jnp.arange(HIST + STRETCH, dtype=jnp.int32)
    allowed = key_pos[None, :] <= query_pos[:, None]

    def one_head(number):
        start = (number * HEAD).astype(jnp.int32)
        queries = lax.dynamic_slice_in_dim(att_query, start, HEAD, 1)
        head_keys = lax.dynamic_slice_in_dim(keys, start, HEAD, 1)
        head_values = lax.dynamic_slice_in_dim(values, start, HEAD, 1)
        scores = jnp.dot(queries, head_keys.T, preferred_element_type=jnp.float32) * (HEAD ** -0.5)
        scores = jnp.where(allowed, scores, NEGATIVE)
        highest = jnp.max(scores, axis=1)
        weights = jnp.where(allowed, jnp.exp(scores - highest[:, None]), 0.0)
        total = jnp.sum(weights, axis=1)
        summed = jnp.dot(weights.astype(jnp.bfloat16), head_values, preferred_element_type=jnp.float32)
        return (summed / total[:, None]).astype(jnp.bfloat16)

    heads_out = lax.map(one_head, jnp.arange(HEADS, dtype=jnp.int32))
    return jnp.transpose(heads_out, (1, 0, 2)).reshape(STRETCH, D)
```

```python
import functools

import jax
import jax.numpy as jnp
from jax import lax
from jax.experimental import pallas as pl
from jax.experimental.pallas import tpu as pltpu
from jax.sharding import PartitionSpec as P

HEAD = 128


NEGATIVE = -1e30


def split_heads(block):
    return block.reshape(block.shape[0], block.shape[1] // HEAD, HEAD)


def absorb(state, queries, query_pos, keys, values, key_pos):
    maxima, totals, sums = state
    scores = jnp.einsum(
        "hqd,khd->hqk", queries, keys, preferred_element_type=jnp.float32
    ) * HEAD ** (-0.5)
    allowed = key_pos[None, None, :] <= query_pos[None, :, None]
    scores = jnp.where(allowed, scores, NEGATIVE)
    newmax = jnp.maximum(maxima, jnp.max(scores, axis=2))
    factor = jnp.exp(maxima - newmax)
    weights = jnp.where(allowed, jnp.exp(scores - newmax[:, :, None]), 0.0)
    totals = totals * factor + jnp.sum(weights, axis=2)
    sums = sums * factor[:, :, None] + jnp.einsum(
        "hqk,khd->hqd", weights.astype(jnp.bfloat16), values, preferred_element_type=jnp.float32
    )
    return (newmax, totals, sums)


def absorb_when_needed(state, queries, query_pos, keys, values, key_pos):
    return lax.cond(
        jnp.min(key_pos) > jnp.max(query_pos),
        lambda carried: carried,
        lambda carried: absorb(carried, queries, query_pos, keys, values, key_pos),
        state,
    )


def finish(state):
    maxima, totals, sums = state
    result = sums / totals[:, :, None]
    return jnp.transpose(result, (1, 0, 2)).reshape(result.shape[1], -1).astype(jnp.bfloat16)


def empty_state(head_count, count):
    return (
        jnp.full((head_count, count), NEGATIVE, jnp.float32),
        jnp.zeros((head_count, count), jnp.float32),
        jnp.zeros((head_count, count, HEAD), jnp.float32),
    )


def local_xla(att_query, att_key, att_value, past_key, past_value):
    seq_count = lax.axis_size("seq")
    position = lax.axis_index("seq")
    past_keys, past_values = (
        lax.all_to_all(past_key, "tp", split_axis=1, concat_axis=0, tiled=True),
        lax.all_to_all(past_value, "tp", split_axis=1, concat_axis=0, tiled=True),
    )
    past_rows = past_keys.shape[0]
    hist_total = past_rows * seq_count
    rows = att_query.shape[0]
    heads_here = att_query.shape[1] // HEAD
    per_device = max(1, heads_here // seq_count)
    repeat = max(1, seq_count // heads_here)
    span = past_rows + rows

    def spread(block):
        return jnp.tile(split_heads(block), (1, repeat, 1))

    stacked_keys = jnp.concatenate([past_keys, att_key], 0)
    stacked_values = jnp.concatenate([past_values, att_value], 0)
    got_query, got_keys, got_values = (
        lax.all_to_all(spread(att_query), "seq", split_axis=1, concat_axis=0, tiled=True),
        lax.all_to_all(spread(stacked_keys), "seq", split_axis=1, concat_axis=0, tiled=True),
        lax.all_to_all(spread(stacked_values), "seq", split_axis=1, concat_axis=0, tiled=True),
    )
    stretch_total = rows * seq_count
    copy_index = position // heads_here
    piece = stretch_total // (2 * repeat)
    first_start = copy_index * piece
    second_start = (2 * repeat - 1 - copy_index) * piece
    offsets = jnp.arange(piece, dtype=jnp.int32)
    pos_one = hist_total + first_start + offsets
    pos_two = hist_total + second_start + offsets
    query_one = jnp.transpose(lax.dynamic_slice_in_dim(got_query, first_start, piece, 0), (1, 0, 2))
    query_two = jnp.transpose(
        lax.dynamic_slice_in_dim(got_query, second_start, piece, 0), (1, 0, 2)
    )
    source = jnp.arange(seq_count, dtype=jnp.int32)[:, None]
    within = jnp.arange(span, dtype=jnp.int32)[None, :]
    key_table = jnp.where(
        within < past_rows,
        source * past_rows + within,
        hist_total + source * rows + within - past_rows,
    )
    turns = seq_count // 2
    key_blocks = got_keys.reshape(turns, 2 * span, per_device, HEAD)
    value_blocks = got_values.reshape(turns, 2 * span, per_device, HEAD)
    pos_blocks = key_table.reshape(turns, 2 * span)

    def step_block(carry_now, items):
        keys, values, key_pos = items
        return (
            (
                absorb_when_needed(carry_now[0], query_one, pos_one, keys, values, key_pos),
                absorb_when_needed(carry_now[1], query_two, pos_two, keys, values, key_pos),
            ),
            None,
        )

    start_state = empty_state(per_device, piece)
    carry, unused = lax.scan(
        step_block, (start_state, start_state), (key_blocks, value_blocks, pos_blocks)
    )
    placed = jnp.zeros((stretch_total, per_device * HEAD), jnp.bfloat16)
    placed = lax.dynamic_update_slice_in_dim(placed, finish(carry[0]), first_start, 0)
    placed = lax.dynamic_update_slice_in_dim(placed, finish(carry[1]), second_start, 0)
    returned = lax.all_to_all(
        placed.reshape(stretch_total, per_device, HEAD),
        "seq",
        split_axis=0,
        concat_axis=1,
        tiled=True,
    )
    summed = jnp.sum(returned.reshape(rows, repeat, heads_here, HEAD).astype(jnp.float32), axis=1)
    return summed.reshape(rows, heads_here * HEAD).astype(jnp.bfloat16)


def attend(query, past_keys, past_values, keys, values):
    rows = query.shape[0]
    contract = (((1,), (1,)), ((), ()))
    past = lax.dot_general(query, past_keys, contract, preferred_element_type=jnp.float32)
    here = lax.dot_general(query, keys, contract, preferred_element_type=jnp.float32)
    free = here.shape[1] - rows
    down = lax.broadcasted_iota(jnp.int32, (rows, rows), 0)
    across = lax.broadcasted_iota(jnp.int32, (rows, rows), 1)
    diagonal = jnp.where(across <= down, here[:, free:], NEGATIVE)
    pieces = [past, diagonal] if free == 0 else [past, here[:, :free], diagonal]
    scores = jnp.concatenate(pieces, 1)
    scale = HEAD ** (-0.5)
    highest = jnp.max(scores, axis=1, keepdims=True)
    weights = jnp.exp((scores - highest) * scale)
    total = jnp.sum(weights, axis=1, keepdims=True)
    rounded = weights.astype(jnp.bfloat16)
    depth = past_keys.shape[0]
    summed = jnp.dot(rounded[:, :depth], past_values, preferred_element_type=jnp.float32)
    summed += jnp.dot(rounded[:, depth:], values, preferred_element_type=jnp.float32)
    return (summed / total).astype(jnp.bfloat16)


def exchange_kernel(
    seqs, tps, q_ref, k_ref, v_ref, pk_ref, pv_ref, o_ref,
    hist, hist_tp, hist_all, past_k, past_v, q_buf, k_buf, v_buf, o_buf,
    tp_send, tp_recv, hist_send, hist_recv, send, recv, o_send, o_recv,
):
    me = lax.axis_index("seq")
    mine = lax.axis_index("tp")
    rows, wide = q_ref.shape
    width = wide // seqs
    heads = width // HEAD

    barrier = pltpu.get_barrier_semaphore()
    for off in range(1, seqs):
        pl.semaphore_signal(
            barrier, inc=1, device_id={"seq": lax.rem(me + off, seqs)},
            device_id_type=pl.DeviceIdType.MESH,
        )
    for off in range(1, tps):
        pl.semaphore_signal(
            barrier, inc=1, device_id={"tp": lax.rem(mine + off, tps)},
            device_id_type=pl.DeviceIdType.MESH,
        )
    for part in range(tps):
        at = slice(part * wide, (part + 1) * wide)
        both = [pk_ref[:, at].astype(jnp.float32), pv_ref[:, at].astype(jnp.float32)]
        hist[part] = jnp.concatenate(both, 0).astype(jnp.bfloat16)
    pl.semaphore_wait(barrier, seqs + tps - 2)

    def columns(number):
        return pl.ds(pl.multiple_of(number * width, width), width)

    sent = []
    for off in range(1, tps):
        other = lax.rem(mine + off, tps)
        copy = pltpu.make_async_remote_copy(
            src_ref=hist.at[other], dst_ref=hist_tp.at[mine],
            send_sem=tp_send.at[off], recv_sem=tp_recv.at[mine],
            device_id={"tp": other}, device_id_type=pl.DeviceIdType.MESH,
        )
        copy.start()
        sent.append(copy)
    pltpu.make_async_copy(hist.at[mine], hist_tp.at[mine], tp_recv.at[mine]).start()
    tensors = ((k_ref, k_buf), (q_ref, q_buf), (v_ref, v_buf))
    for number, (ref, buf) in enumerate(tensors):
        for off in range(1, seqs):
            other = lax.rem(me + off, seqs)
            copy = pltpu.make_async_remote_copy(
                src_ref=ref.at[:, columns(other)], dst_ref=buf.at[me],
                send_sem=send.at[number, off], recv_sem=recv.at[number, me],
                device_id={"seq": other}, device_id_type=pl.DeviceIdType.MESH,
            )
            copy.start()
            sent.append(copy)
        pltpu.make_async_copy(ref.at[:, columns(me)], buf.at[me], recv.at[number, me]).start()
    for part in range(tps):
        pltpu.make_async_copy(hist_tp.at[part], hist_tp.at[part], tp_recv.at[part]).wait()
    for off in range(1, seqs):
        other = lax.rem(me + off, seqs)
        copy = pltpu.make_async_remote_copy(
            src_ref=hist_tp.at[:, :, columns(other)], dst_ref=hist_all.at[me],
            send_sem=hist_send.at[off], recv_sem=hist_recv.at[me],
            device_id={"seq": other}, device_id_type=pl.DeviceIdType.MESH,
        )
        copy.start()
        sent.append(copy)
    pltpu.make_async_copy(hist_tp.at[:, :, columns(me)], hist_all.at[me], hist_recv.at[me]).start()

    for source in range(seqs):
        pltpu.make_async_copy(hist_all.at[source], hist_all.at[source], hist_recv.at[source]).wait()
        half = hist_all.shape[2] // 2
        blocks = [hist_all[source, part].astype(jnp.float32) for part in range(tps)]
        at = slice(source * tps * half, (source + 1) * tps * half)
        past_k[at, :] = jnp.concatenate([b[:half] for b in blocks], 0).astype(jnp.bfloat16)
        past_v[at, :] = jnp.concatenate([b[half:] for b in blocks], 0).astype(jnp.bfloat16)

    for block in range(seqs):
        for number, (ref, buf) in enumerate(tensors):
            pltpu.make_async_copy(buf.at[block], buf.at[block], recv.at[number, block]).wait()
        count = (block + 1) * rows
        for head in range(heads):
            at = slice(head * HEAD, (head + 1) * HEAD)
            o_buf[block, :, at] = attend(
                q_buf[block, :, at],
                past_k[:, at],
                past_v[:, at],
                k_buf[: block + 1, :, at].reshape(count, HEAD),
                v_buf[: block + 1, :, at].reshape(count, HEAD),
            )

        @pl.when(me != block)
        def _():
            pltpu.make_async_remote_copy(
                src_ref=o_buf.at[block], dst_ref=o_ref.at[:, columns(me)],
                send_sem=o_send.at[block], recv_sem=o_recv.at[me],
                device_id={"seq": block}, device_id_type=pl.DeviceIdType.MESH,
            ).start()

        @pl.when(me == block)
        def _():
            pltpu.make_async_copy(o_buf.at[block], o_ref.at[:, columns(me)], o_recv.at[me]).start()

    for copy in sent:
        copy.wait_send()
    for block in range(seqs):
        spot = o_ref.at[:, block * width : (block + 1) * width]
        pltpu.make_async_copy(spot, spot, o_recv.at[block]).wait()

        @pl.when(me != block)
        def _():
            pltpu.make_async_copy(o_buf.at[block], o_buf.at[block], o_send.at[block]).wait()


def local_kernel(seqs, tps, att_query, att_key, att_value, past_key, past_value):
    rows, wide = att_query.shape
    width = wide // seqs
    past_rows = past_key.shape[0]
    depth = past_rows * seqs * tps
    anywhere = pl.BlockSpec(memory_space=pl.ANY)
    near = pl.BlockSpec(memory_space=pltpu.VMEM)
    bf16 = jnp.bfloat16
    dma = pltpu.SemaphoreType.DMA
    return pl.pallas_call(
        functools.partial(exchange_kernel, seqs, tps),
        out_shape=jax.ShapeDtypeStruct((rows, wide), bf16),
        in_specs=[anywhere, anywhere, anywhere, near, near],
        out_specs=near,
        scratch_shapes=[
            pltpu.VMEM((tps, 2 * past_rows, wide), bf16),
            pltpu.VMEM((tps, 2 * past_rows, wide), bf16),
            pltpu.VMEM((seqs, tps, 2 * past_rows, width), bf16),
            pltpu.VMEM((depth, width), bf16),
            pltpu.VMEM((depth, width), bf16),
            pltpu.VMEM((seqs, rows, width), bf16),
            pltpu.VMEM((seqs, rows, width), bf16),
            pltpu.VMEM((seqs, rows, width), bf16),
            pltpu.VMEM((seqs, rows, width), bf16),
            dma((tps,)),
            dma((tps,)),
            dma((seqs,)),
            dma((seqs,)),
            dma((3, seqs)),
            dma((3, seqs)),
            dma((seqs,)),
            dma((seqs,)),
        ],
        compiler_params=pltpu.CompilerParams(
            collective_id=0, has_side_effects=True, vmem_limit_bytes=40 * 2**20
        ),
    )(att_query, att_key, att_value, past_key, past_value)


def local(att_query, att_key, att_value, past_key, past_value):
    seqs, tps = lax.axis_size("seq"), lax.axis_size("tp")
    rows, wide = att_query.shape
    fits = wide % (seqs * HEAD) == 0 and wide * tps == past_key.shape[1]
    if fits and past_key.shape[0] == 8 and rows % 16 == 0 and rows <= 256 and seqs <= 8:
        return local_kernel(seqs, tps, att_query, att_key, att_value, past_key, past_value)
    return local_xla(att_query, att_key, att_value, past_key, past_value)


def solution(mesh):
    placed = (
        P("seq", "tp"),
        P("seq", "tp"),
        P("seq", "tp"),
        P(("seq", "tp"), None),
        P(("seq", "tp"), None),
    )
    return jax.shard_map(
        local, mesh=mesh, in_specs=placed, out_specs=P("seq", "tp"), check_vma=False
    )
```

```python
import functools

import jax
import jax.numpy as jnp
from jax import lax
from jax.experimental import pallas as pl
from jax.experimental.pallas import tpu as pltpu
from jax.sharding import PartitionSpec as P

HEAD = 128


NEGATIVE = -1e30


def split_heads(block):
    return block.reshape(block.shape[0], block.shape[1] // HEAD, HEAD)


def absorb(state, queries, query_pos, keys, values, key_pos):
    maxima, totals, sums = state
    scores = jnp.einsum(
        "hqd,khd->hqk", queries, keys, preferred_element_type=jnp.float32
    ) * HEAD ** (-0.5)
    allowed = key_pos[None, None, :] <= query_pos[None, :, None]
    scores = jnp.where(allowed, scores, NEGATIVE)
    newmax = jnp.maximum(maxima, jnp.max(scores, axis=2))
    factor = jnp.exp(maxima - newmax)
    weights = jnp.where(allowed, jnp.exp(scores - newmax[:, :, None]), 0.0)
    totals = totals * factor + jnp.sum(weights, axis=2)
    sums = sums * factor[:, :, None] + jnp.einsum(
        "hqk,khd->hqd", weights.astype(jnp.bfloat16), values, preferred_element_type=jnp.float32
    )
    return (newmax, totals, sums)


def absorb_when_needed(state, queries, query_pos, keys, values, key_pos):
    return lax.cond(
        jnp.min(key_pos) > jnp.max(query_pos),
        lambda carried: carried,
        lambda carried: absorb(carried, queries, query_pos, keys, values, key_pos),
        state,
    )


def finish(state):
    maxima, totals, sums = state
    result = sums / totals[:, :, None]
    return jnp.transpose(result, (1, 0, 2)).reshape(result.shape[1], -1).astype(jnp.bfloat16)


def empty_state(head_count, count):
    return (
        jnp.full((head_count, count), NEGATIVE, jnp.float32),
        jnp.zeros((head_count, count), jnp.float32),
        jnp.zeros((head_count, count, HEAD), jnp.float32),
    )


def local_xla(att_query, att_key, att_value, past_key, past_value):
    seq_count = lax.axis_size("seq")
    position = lax.axis_index("seq")
    past_keys, past_values = (
        lax.all_to_all(past_key, "tp", split_axis=1, concat_axis=0, tiled=True),
        lax.all_to_all(past_value, "tp", split_axis=1, concat_axis=0, tiled=True),
    )
    past_rows = past_keys.shape[0]
    hist_total = past_rows * seq_count
    rows = att_query.shape[0]
    heads_here = att_query.shape[1] // HEAD
    per_device = max(1, heads_here // seq_count)
    repeat = max(1, seq_count // heads_here)
    span = past_rows + rows

    def spread(block):
        return jnp.tile(split_heads(block), (1, repeat, 1))

    stacked_keys = jnp.concatenate([past_keys, att_key], 0)
    stacked_values = jnp.concatenate([past_values, att_value], 0)
    got_query, got_keys, got_values = (
        lax.all_to_all(spread(att_query), "seq", split_axis=1, concat_axis=0, tiled=True),
        lax.all_to_all(spread(stacked_keys), "seq", split_axis=1, concat_axis=0, tiled=True),
        lax.all_to_all(spread(stacked_values), "seq", split_axis=1, concat_axis=0, tiled=True),
    )
    stretch_total = rows * seq_count
    copy_index = position // heads_here
    piece = stretch_total // (2 * repeat)
    first_start = copy_index * piece
    second_start = (2 * repeat - 1 - copy_index) * piece
    offsets = jnp.arange(piece, dtype=jnp.int32)
    pos_one = hist_total + first_start + offsets
    pos_two = hist_total + second_start + offsets
    query_one = jnp.transpose(lax.dynamic_slice_in_dim(got_query, first_start, piece, 0), (1, 0, 2))
    query_two = jnp.transpose(
        lax.dynamic_slice_in_dim(got_query, second_start, piece, 0), (1, 0, 2)
    )
    source = jnp.arange(seq_count, dtype=jnp.int32)[:, None]
    within = jnp.arange(span, dtype=jnp.int32)[None, :]
    key_table = jnp.where(
        within < past_rows,
        source * past_rows + within,
        hist_total + source * rows + within - past_rows,
    )
    turns = seq_count // 2
    key_blocks = got_keys.reshape(turns, 2 * span, per_device, HEAD)
    value_blocks = got_values.reshape(turns, 2 * span, per_device, HEAD)
    pos_blocks = key_table.reshape(turns, 2 * span)

    def step_block(carry_now, items):
        keys, values, key_pos = items
        return (
            (
                absorb_when_needed(carry_now[0], query_one, pos_one, keys, values, key_pos),
                absorb_when_needed(carry_now[1], query_two, pos_two, keys, values, key_pos),
            ),
            None,
        )

    start_state = empty_state(per_device, piece)
    carry, unused = lax.scan(
        step_block, (start_state, start_state), (key_blocks, value_blocks, pos_blocks)
    )
    placed = jnp.zeros((stretch_total, per_device * HEAD), jnp.bfloat16)
    placed = lax.dynamic_update_slice_in_dim(placed, finish(carry[0]), first_start, 0)
    placed = lax.dynamic_update_slice_in_dim(placed, finish(carry[1]), second_start, 0)
    returned = lax.all_to_all(
        placed.reshape(stretch_total, per_device, HEAD),
        "seq",
        split_axis=0,
        concat_axis=1,
        tiled=True,
    )
    summed = jnp.sum(returned.reshape(rows, repeat, heads_here, HEAD).astype(jnp.float32), axis=1)
    return summed.reshape(rows, heads_here * HEAD).astype(jnp.bfloat16)


SCALE = HEAD ** (-0.5)
CHUNKS = 4


def partial(query, pieces, diagonal):
    contract = (((1,), (1,)), ((), ()))
    found = [
        lax.dot_general(keys, query, contract, preferred_element_type=jnp.float32)
        for keys, values in pieces
    ]
    if diagonal:
        shape = found[-1].shape
        key_at = lax.broadcasted_iota(jnp.int32, shape, 0)
        query_at = lax.broadcasted_iota(jnp.int32, shape, 1)
        found[-1] = jnp.where(key_at <= query_at, found[-1], NEGATIVE)
    highest = functools.reduce(
        jnp.maximum, [jnp.max(scores, axis=0, keepdims=True) for scores in found]
    )
    total = jnp.zeros_like(highest)
    summed = jnp.zeros((HEAD, query.shape[0]), jnp.float32)
    for scores, (keys, values) in zip(found, pieces):
        weights = jnp.exp((scores - highest) * SCALE)
        total += jnp.sum(weights, axis=0, keepdims=True)
        summed += lax.dot_general(
            values, weights.astype(jnp.bfloat16), (((0,), (0,)), ((), ())),
            preferred_element_type=jnp.float32,
        )
    return summed / total, highest * SCALE + jnp.log(total)


def merge(parts):
    top = functools.reduce(jnp.maximum, [level for rows, level in parts])
    shares = [jnp.exp(level - top) for rows, level in parts]
    out = sum(rows * share for (rows, level), share in zip(parts, shares))
    return out / sum(shares)


def wait(ref, sem):
    pltpu.make_async_copy(ref, ref, sem).wait()


def chain_kernel(
    tps, q_ref, k_ref, v_ref, pk_ref, pv_ref, o_ref,
    hist, hist_tp, slab, past_k, past_v, own, far_q, far_kv, got_o, got_l, give_o, give_l,
    keep_o, keep_l, o_buf,
    tp_send, tp_recv, hy_send, hy_recv, hz_send, hz_recv, own_send, own_recv,
    far_send, far_q_recv, far_kv_recv, go_send, go_recv, gl_send, gl_recv, fin_send, fin_recv,
):
    seqs, zs = 8, 4
    me = lax.axis_index("seq")
    mine = lax.axis_index("tp")
    z, y = me // 2, lax.rem(me, 2)
    peer = z * 2 + 1 - y
    rows, wide = q_ref.shape
    half = wide // 2
    width = half // CHUNKS
    heads = width // HEAD
    mesh_id = pl.DeviceIdType.MESH

    barrier = pltpu.get_barrier_semaphore()
    for off in range(1, seqs):
        pl.semaphore_signal(
            barrier, inc=1, device_id={"seq": lax.rem(me + off, seqs)}, device_id_type=mesh_id
        )
    for off in range(1, tps):
        pl.semaphore_signal(
            barrier, inc=1, device_id={"tp": lax.rem(mine + off, tps)}, device_id_type=mesh_id
        )
    for part in range(tps):
        at = slice(part * wide, (part + 1) * wide)
        both = [pk_ref[:, at].astype(jnp.float32), pv_ref[:, at].astype(jnp.float32)]
        hist[part] = jnp.concatenate(both, 0).astype(jnp.bfloat16)
    pl.semaphore_wait(barrier, seqs + tps - 2)

    def columns(side, chunk):
        return pl.ds(pl.multiple_of(side * half + chunk * width, width), width)

    def send_to(seq, src, dst, send_sem, recv_sem):
        pltpu.make_async_remote_copy(
            src_ref=src, dst_ref=dst, send_sem=send_sem, recv_sem=recv_sem,
            device_id={"seq": seq}, device_id_type=mesh_id,
        ).start()

    for off in range(1, tps):
        other = lax.rem(mine + off, tps)
        pltpu.make_async_remote_copy(
            src_ref=hist.at[other], dst_ref=hist_tp.at[mine],
            send_sem=tp_send.at[off], recv_sem=tp_recv.at[mine],
            device_id={"tp": other}, device_id_type=mesh_id,
        ).start()
    pltpu.make_async_copy(hist.at[mine], hist_tp.at[mine], tp_recv.at[mine]).start()

    def send_far(chunk):
        @pl.when(z == 0)
        def _():
            for side in range(2):
                for kind, ref in enumerate((k_ref, v_ref)):
                    send_to(
                        2 + side, ref.at[:, columns(side, chunk)], far_kv.at[kind, y, chunk],
                        far_send.at[kind, side, chunk], far_kv_recv.at[kind, y, chunk],
                    )

        @pl.when(z == 2)
        def _():
            for side in range(2):
                send_to(
                    2 + side, q_ref.at[:, columns(side, chunk)], far_q.at[0, y, chunk],
                    far_send.at[0, side, chunk], far_q_recv.at[0, y, chunk],
                )

        @pl.when(z == 3)
        def _():
            for target in range(2):
                for side in range(2):
                    send_to(
                        2 + 2 * target + side, q_ref.at[:, columns(side, chunk)],
                        far_q.at[1, y, chunk],
                        far_send.at[target, side, chunk], far_q_recv.at[1, y, chunk],
                    )

    def send_own(chunk):
        for kind, ref in enumerate((q_ref, k_ref, v_ref)):
            send_to(
                peer, ref.at[:, columns(1 - y, chunk)], own.at[kind, y, chunk],
                own_send.at[kind, chunk], own_recv.at[kind, y, chunk],
            )
            pltpu.make_async_copy(
                ref.at[:, columns(y, chunk)], own.at[kind, y, chunk], own_recv.at[kind, y, chunk]
            ).start()

    send_far(0)
    send_own(0)
    for part in range(tps):
        wait(hist_tp.at[part], tp_recv.at[part])
    away = hist_tp.at[:, :, pl.ds(pl.multiple_of((1 - y) * half, half), half)]
    here = hist_tp.at[:, :, pl.ds(pl.multiple_of(y * half, half), half)]
    send_to(peer, away, slab.at[z, y], hy_send.at[0], hy_recv.at[y])
    pltpu.make_async_copy(here, slab.at[z, y], hy_recv.at[y]).start()
    send_far(1)
    for side in range(2):
        wait(slab.at[z, side], hy_recv.at[side])

    def pass_slab(number, target):
        send_to(
            target * 2 + y, slab.at[number], slab.at[number], hz_send.at[number], hz_recv.at[number]
        )

    for origin in range(zs):
        pl.when(z == origin)(
            functools.partial(pass_slab, origin, 1 if origin == 0 else origin - 1)
        )

    @pl.when(z == 2)
    def _():
        wait(slab.at[3], hz_recv.at[3])
        pass_slab(3, 1)

    for chunk in range(1, CHUNKS):
        if chunk > 1:
            send_far(chunk)
        send_own(chunk)

    def settle(number):
        past_rows = slab.shape[3] // 2
        count = 2 * tps * past_rows
        at = slice(number * count, (number + 1) * count)
        for chunk in range(CHUNKS):
            cut = slice(chunk * width, (chunk + 1) * width)
            blocks = [
                slab[number, side, part, :, cut].astype(jnp.float32)
                for side in range(2)
                for part in range(tps)
            ]
            past_k[chunk, at] = jnp.concatenate([b[:past_rows] for b in blocks], 0).astype(jnp.bfloat16)
            past_v[chunk, at] = jnp.concatenate([b[past_rows:] for b in blocks], 0).astype(jnp.bfloat16)

    def lanes(head):
        return slice(head * HEAD, (head + 1) * HEAD)

    def own_of(kind, chunk, head):
        return own[kind, :, chunk, :, lanes(head)].reshape(2 * rows, HEAD)

    def far_q_of(slot, chunk, head):
        return far_q[slot, :, chunk, :, lanes(head)].reshape(2 * rows, HEAD)

    def near_pair(chunk, head):
        return own_of(1, chunk, head), own_of(2, chunk, head)

    def far_pair(chunk, head):
        return tuple(
            far_kv[kind, :, chunk, :, lanes(head)].reshape(2 * rows, HEAD) for kind in range(2)
        )

    def past_pair(chunk, head, first, last):
        at = slice(first * past_k.shape[1] // zs, last * past_k.shape[1] // zs)
        return past_k[chunk, at, lanes(head)], past_v[chunk, at, lanes(head)]

    def wait_own(chunk):
        for kind in range(3):
            for side in range(2):
                wait(own.at[kind, side, chunk], own_recv.at[kind, side, chunk])

    def wait_far_q(slot, chunk):
        for side in range(2):
            wait(far_q.at[slot, side, chunk], far_q_recv.at[slot, side, chunk])

    def give(slot, target, source, chunk):
        send_to(
            target * 2 + y, give_o.at[slot, chunk], got_o.at[source, chunk],
            go_send.at[slot, chunk], go_recv.at[source, chunk],
        )
        send_to(
            target * 2 + y, give_l.at[slot, chunk], got_l.at[source, chunk],
            gl_send.at[slot, chunk], gl_recv.at[source, chunk],
        )

    def put_part(slot, chunk, head, part):
        give_o[slot, chunk, head] = part[0].astype(jnp.bfloat16)
        give_l[slot, chunk, head] = jnp.broadcast_to(part[1], give_l.shape[3:])

    def put_result(chunk, head, result):
        flat = jnp.transpose(result).astype(jnp.bfloat16)
        for side in range(2):
            o_buf[chunk, side, :, lanes(head)] = flat[side * rows : (side + 1) * rows]

    def finish_chunk(chunk):
        spot = o_ref.at[:, columns(y, chunk)]
        send_to(peer, o_buf.at[chunk, 1 - y], spot, fin_send.at[chunk], fin_recv.at[y, chunk])
        pltpu.make_async_copy(o_buf.at[chunk, y], spot, fin_recv.at[y, chunk]).start()

    def each_chunk(first, body):
        def step(chunk, unused):
            body(chunk)
            return unused

        lax.fori_loop(first, CHUNKS, step, 0)

    def wait_slabs(numbers):
        for number in numbers:
            wait(slab.at[number], hz_recv.at[number])

    def sent_slabs(numbers):
        for number in numbers:
            wait(slab.at[number], hz_send.at[number])

    def sent_far(targets, sides):
        def body(chunk):
            for target in range(targets):
                for side in range(sides):
                    wait(far_q.at[0, 0, 0], far_send.at[target, side, chunk])

        each_chunk(0, body)

    def sent_parts(slots):
        def body(chunk):
            for slot in slots:
                wait(give_o.at[slot, chunk], go_send.at[slot, chunk])
                wait(give_l.at[slot, chunk], gl_send.at[slot, chunk])

        each_chunk(0, body)

    @pl.when(z == 0)
    def _():
        wait_slabs((1, 2, 3))
        for number in range(zs):
            settle(number)

        def body(chunk):
            wait_own(chunk)
            for head in range(heads):
                pieces = [past_pair(chunk, head, 0, zs), near_pair(chunk, head)]
                put_result(chunk, head, partial(own_of(0, chunk, head), pieces, True)[0])
            finish_chunk(chunk)

        each_chunk(0, body)
        sent_slabs((0,))
        sent_far(2, 2)

    @pl.when(z == 1)
    def _():
        wait_slabs((0,))
        settle(0)
        settle(1)

        def far_part(chunk):
            wait_own(chunk)
            for kind in range(2):
                for side in range(2):
                    wait(far_kv.at[kind, side, chunk], far_kv_recv.at[kind, side, chunk])
            for slot in (1, 0):
                wait_far_q(slot, chunk)
                for head in range(heads):
                    pieces = [
                        past_pair(chunk, head, 0, 2), far_pair(chunk, head), near_pair(chunk, head)
                    ]
                    put_part(slot, chunk, head, partial(far_q_of(slot, chunk, head), pieces, False))
                give(slot, 2 + slot, 0, chunk)

        def own_part(chunk):
            for head in range(heads):
                pieces = [
                    past_pair(chunk, head, 0, zs), far_pair(chunk, head), near_pair(chunk, head)
                ]
                put_result(chunk, head, partial(own_of(0, chunk, head), pieces, True)[0])
            finish_chunk(chunk)

        def body(chunk):
            far_part(chunk)

            @pl.when(chunk == 0)
            def _():
                for number in (2, 3):
                    wait_slabs((number,))
                    pass_slab(number, 0)
                    settle(number)

            own_part(chunk)

        each_chunk(0, body)
        sent_slabs((1, 2, 3))
        sent_parts((0, 1))

    def keep(chunk, head, part):
        keep_o[chunk, head] = part[0]
        keep_l[chunk, head] = jnp.broadcast_to(part[1], keep_l.shape[2:])

    def combine(sources):
        def body(chunk):
            for source in sources:
                wait(got_o.at[source, chunk], go_recv.at[source, chunk])
                wait(got_l.at[source, chunk], gl_recv.at[source, chunk])
            for head in range(heads):
                parts = [(keep_o[chunk, head], keep_l[chunk, head, :1])]
                for source in sources:
                    parts.append(
                        (
                            got_o[source, chunk, head].astype(jnp.float32),
                            got_l[source, chunk, head, :1],
                        )
                    )
                put_result(chunk, head, merge(parts))
            finish_chunk(chunk)

        each_chunk(0, body)

    @pl.when(z == 2)
    def _():
        settle(2)
        settle(3)

        def body(chunk):
            wait_own(chunk)
            wait_far_q(1, chunk)
            for head in range(heads):
                pieces = [past_pair(chunk, head, 2, zs), near_pair(chunk, head)]
                put_part(1, chunk, head, partial(far_q_of(1, chunk, head), pieces, False))
            give(1, 3, 1, chunk)
            for head in range(heads):
                pieces = [past_pair(chunk, head, 2, zs), near_pair(chunk, head)]
                keep(chunk, head, partial(own_of(0, chunk, head), pieces, True))

        each_chunk(0, body)
        combine((0,))
        sent_slabs((2, 3))
        sent_far(1, 2)
        sent_parts((1,))

    @pl.when(z == 3)
    def _():
        def body(chunk):
            wait_own(chunk)
            for head in range(heads):
                keep(chunk, head, partial(own_of(0, chunk, head), [near_pair(chunk, head)], True))

        each_chunk(0, body)
        combine((0, 1))
        sent_slabs((3,))
        sent_far(2, 2)

    for off in range(1, tps):
        wait(hist.at[0], tp_send.at[off])
    wait(slab.at[0, 0], hy_send.at[0])

    def last(chunk):
        for kind in range(3):
            wait(own.at[kind, 0, chunk], own_send.at[kind, chunk])
        wait(o_buf.at[chunk, 0], fin_send.at[chunk])
        for side in range(2):
            wait(o_ref.at[:, columns(side, chunk)], fin_recv.at[side, chunk])

    each_chunk(0, last)


def local_chain(tps, att_query, att_key, att_value, past_key, past_value):
    rows, wide = att_query.shape
    half = wide // 2
    width = half // CHUNKS
    heads = width // HEAD
    past_rows = past_key.shape[0]
    depth = past_rows * 8 * tps
    far = pl.BlockSpec(memory_space=pltpu.HBM)
    near = pl.BlockSpec(memory_space=pltpu.VMEM)
    dma = pltpu.SemaphoreType.DMA

    def held(*shape):
        return pltpu.VMEM(shape, jnp.bfloat16)

    def wider(*shape):
        return pltpu.VMEM(shape, jnp.float32)

    return pl.pallas_call(
        functools.partial(chain_kernel, tps),
        out_shape=jax.ShapeDtypeStruct((rows, wide), jnp.bfloat16),
        in_specs=[far, far, far, near, near],
        out_specs=near,
        scratch_shapes=[
            held(tps, 2 * past_rows, wide),
            held(tps, 2 * past_rows, wide),
            held(4, 2, tps, 2 * past_rows, half),
            held(CHUNKS, depth, width),
            held(CHUNKS, depth, width),
            held(3, 2, CHUNKS, rows, width),
            held(2, 2, CHUNKS, rows, width),
            held(2, 2, CHUNKS, rows, width),
            held(2, CHUNKS, heads, HEAD, 2 * rows),
            wider(2, CHUNKS, heads, 8, 2 * rows),
            held(2, CHUNKS, heads, HEAD, 2 * rows),
            wider(2, CHUNKS, heads, 8, 2 * rows),
            wider(CHUNKS, heads, HEAD, 2 * rows),
            wider(CHUNKS, heads, 8, 2 * rows),
            held(CHUNKS, 2, rows, width),
            dma((tps,)),
            dma((tps,)),
            dma((1,)),
            dma((2,)),
            dma((4,)),
            dma((4,)),
            dma((3, CHUNKS)),
            dma((3, 2, CHUNKS)),
            dma((2, 2, CHUNKS)),
            dma((2, 2, CHUNKS)),
            dma((2, 2, CHUNKS)),
            dma((2, CHUNKS)),
            dma((2, CHUNKS)),
            dma((2, CHUNKS)),
            dma((2, CHUNKS)),
            dma((CHUNKS,)),
            dma((2, CHUNKS)),
        ],
        compiler_params=pltpu.CompilerParams(
            collective_id=0, has_side_effects=True, vmem_limit_bytes=56 * 2**20
        ),
    )(att_query, att_key, att_value, past_key, past_value)


def local(att_query, att_key, att_value, past_key, past_value):
    seqs, tps = lax.axis_size("seq"), lax.axis_size("tp")
    rows, wide = att_query.shape
    fits = wide % (2 * CHUNKS * HEAD) == 0 and wide * tps == past_key.shape[1]
    if seqs == 8 and fits and past_key.shape[0] == 8 and rows == 128:
        return local_chain(tps, att_query, att_key, att_value, past_key, past_value)
    return local_xla(att_query, att_key, att_value, past_key, past_value)


def solution(mesh):
    placed = (
        P("seq", "tp"),
        P("seq", "tp"),
        P("seq", "tp"),
        P(("seq", "tp"), None),
        P(("seq", "tp"), None),
    )
    return jax.shard_map(
        local, mesh=mesh, in_specs=placed, out_specs=P("seq", "tp"), check_vma=False
    )
```

```python
import functools

import jax
import jax.numpy as jnp
from jax import lax
from jax.experimental import pallas as pl
from jax.experimental.pallas import tpu as pltpu
from jax.sharding import PartitionSpec as P

HEAD = 128


NEGATIVE = -1e30


def split_heads(block):
    return block.reshape(block.shape[0], block.shape[1] // HEAD, HEAD)


def absorb(state, queries, query_pos, keys, values, key_pos):
    maxima, totals, sums = state
    scores = jnp.einsum(
        "hqd,khd->hqk", queries, keys, preferred_element_type=jnp.float32
    ) * HEAD ** (-0.5)
    allowed = key_pos[None, None, :] <= query_pos[None, :, None]
    scores = jnp.where(allowed, scores, NEGATIVE)
    newmax = jnp.maximum(maxima, jnp.max(scores, axis=2))
    factor = jnp.exp(maxima - newmax)
    weights = jnp.where(allowed, jnp.exp(scores - newmax[:, :, None]), 0.0)
    totals = totals * factor + jnp.sum(weights, axis=2)
    sums = sums * factor[:, :, None] + jnp.einsum(
        "hqk,khd->hqd", weights.astype(jnp.bfloat16), values, preferred_element_type=jnp.float32
    )
    return (newmax, totals, sums)


def absorb_when_needed(state, queries, query_pos, keys, values, key_pos):
    return lax.cond(
        jnp.min(key_pos) > jnp.max(query_pos),
        lambda carried: carried,
        lambda carried: absorb(carried, queries, query_pos, keys, values, key_pos),
        state,
    )


def finish(state):
    maxima, totals, sums = state
    result = sums / totals[:, :, None]
    return jnp.transpose(result, (1, 0, 2)).reshape(result.shape[1], -1).astype(jnp.bfloat16)


def empty_state(head_count, count):
    return (
        jnp.full((head_count, count), NEGATIVE, jnp.float32),
        jnp.zeros((head_count, count), jnp.float32),
        jnp.zeros((head_count, count, HEAD), jnp.float32),
    )


def local_xla(att_query, att_key, att_value, past_key, past_value):
    seq_count = lax.axis_size("seq")
    position = lax.axis_index("seq")
    past_keys, past_values = (
        lax.all_to_all(past_key, "tp", split_axis=1, concat_axis=0, tiled=True),
        lax.all_to_all(past_value, "tp", split_axis=1, concat_axis=0, tiled=True),
    )
    past_rows = past_keys.shape[0]
    hist_total = past_rows * seq_count
    rows = att_query.shape[0]
    heads_here = att_query.shape[1] // HEAD
    per_device = max(1, heads_here // seq_count)
    repeat = max(1, seq_count // heads_here)
    span = past_rows + rows

    def spread(block):
        return jnp.tile(split_heads(block), (1, repeat, 1))

    stacked_keys = jnp.concatenate([past_keys, att_key], 0)
    stacked_values = jnp.concatenate([past_values, att_value], 0)
    got_query, got_keys, got_values = (
        lax.all_to_all(spread(att_query), "seq", split_axis=1, concat_axis=0, tiled=True),
        lax.all_to_all(spread(stacked_keys), "seq", split_axis=1, concat_axis=0, tiled=True),
        lax.all_to_all(spread(stacked_values), "seq", split_axis=1, concat_axis=0, tiled=True),
    )
    stretch_total = rows * seq_count
    copy_index = position // heads_here
    piece = stretch_total // (2 * repeat)
    first_start = copy_index * piece
    second_start = (2 * repeat - 1 - copy_index) * piece
    offsets = jnp.arange(piece, dtype=jnp.int32)
    pos_one = hist_total + first_start + offsets
    pos_two = hist_total + second_start + offsets
    query_one = jnp.transpose(lax.dynamic_slice_in_dim(got_query, first_start, piece, 0), (1, 0, 2))
    query_two = jnp.transpose(
        lax.dynamic_slice_in_dim(got_query, second_start, piece, 0), (1, 0, 2)
    )
    source = jnp.arange(seq_count, dtype=jnp.int32)[:, None]
    within = jnp.arange(span, dtype=jnp.int32)[None, :]
    key_table = jnp.where(
        within < past_rows,
        source * past_rows + within,
        hist_total + source * rows + within - past_rows,
    )
    turns = seq_count // 2
    key_blocks = got_keys.reshape(turns, 2 * span, per_device, HEAD)
    value_blocks = got_values.reshape(turns, 2 * span, per_device, HEAD)
    pos_blocks = key_table.reshape(turns, 2 * span)

    def step_block(carry_now, items):
        keys, values, key_pos = items
        return (
            (
                absorb_when_needed(carry_now[0], query_one, pos_one, keys, values, key_pos),
                absorb_when_needed(carry_now[1], query_two, pos_two, keys, values, key_pos),
            ),
            None,
        )

    start_state = empty_state(per_device, piece)
    carry, unused = lax.scan(
        step_block, (start_state, start_state), (key_blocks, value_blocks, pos_blocks)
    )
    placed = jnp.zeros((stretch_total, per_device * HEAD), jnp.bfloat16)
    placed = lax.dynamic_update_slice_in_dim(placed, finish(carry[0]), first_start, 0)
    placed = lax.dynamic_update_slice_in_dim(placed, finish(carry[1]), second_start, 0)
    returned = lax.all_to_all(
        placed.reshape(stretch_total, per_device, HEAD),
        "seq",
        split_axis=0,
        concat_axis=1,
        tiled=True,
    )
    summed = jnp.sum(returned.reshape(rows, repeat, heads_here, HEAD).astype(jnp.float32), axis=1)
    return summed.reshape(rows, heads_here * HEAD).astype(jnp.bfloat16)


SCALE = HEAD ** (-0.5)
CHUNKS = 4
AHEAD = 2


def partial(query, pieces, diagonal):
    contract = (((1,), (1,)), ((), ()))
    found = [
        lax.dot_general(keys, query, contract, preferred_element_type=jnp.float32)
        for keys, values in pieces
    ]
    if diagonal:
        shape = found[-1].shape
        key_at = lax.broadcasted_iota(jnp.int32, shape, 0)
        query_at = lax.broadcasted_iota(jnp.int32, shape, 1)
        found[-1] = jnp.where(key_at <= query_at, found[-1], NEGATIVE)
    highest = functools.reduce(
        jnp.maximum, [jnp.max(scores, axis=0, keepdims=True) for scores in found]
    )
    total = jnp.zeros_like(highest)
    summed = jnp.zeros((HEAD, query.shape[0]), jnp.float32)
    for scores, (keys, values) in zip(found, pieces):
        weights = jnp.exp((scores - highest) * SCALE)
        total += jnp.sum(weights, axis=0, keepdims=True)
        summed += lax.dot_general(
            values, weights.astype(jnp.bfloat16), (((0,), (0,)), ((), ())),
            preferred_element_type=jnp.float32,
        )
    return summed / total, highest * SCALE + jnp.log(total)


def merge(parts):
    top = functools.reduce(jnp.maximum, [level for rows, level in parts])
    shares = [jnp.exp(level - top) for rows, level in parts]
    out = sum(rows * share for (rows, level), share in zip(parts, shares))
    return out / sum(shares)


def wait(ref, sem):
    pltpu.make_async_copy(ref, ref, sem).wait()


def chain_kernel(
    tps, q_ref, k_ref, v_ref, pk_ref, pv_ref, o_ref,
    hist, hist_tp, slab, past_k, past_v, own, far_q, far_kv, got_o, got_l, give_o, give_l,
    keep_o, keep_l, o_buf,
    tp_send, tp_recv, hy_send, hy_recv, hz_send, hz_recv, own_send, own_recv,
    far_send, far_q_recv, far_kv_recv, go_send, go_recv, gl_send, gl_recv, fin_send, fin_recv,
):
    seqs, zs = 8, 4
    me = lax.axis_index("seq")
    mine = lax.axis_index("tp")
    z, y = me // 2, lax.rem(me, 2)
    peer = z * 2 + 1 - y
    rows, wide = q_ref.shape
    half = wide // 2
    width = half // CHUNKS
    heads = width // HEAD
    mesh_id = pl.DeviceIdType.MESH

    barrier = pltpu.get_barrier_semaphore()
    for off in range(1, seqs):
        pl.semaphore_signal(
            barrier, inc=1, device_id={"seq": lax.rem(me + off, seqs)}, device_id_type=mesh_id
        )
    for off in range(1, tps):
        pl.semaphore_signal(
            barrier, inc=1, device_id={"tp": lax.rem(mine + off, tps)}, device_id_type=mesh_id
        )
    for part in range(tps):
        at = slice(part * wide, (part + 1) * wide)
        both = [pk_ref[:, at].astype(jnp.float32), pv_ref[:, at].astype(jnp.float32)]
        hist[part] = jnp.concatenate(both, 0).astype(jnp.bfloat16)
    pl.semaphore_wait(barrier, seqs + tps - 2)

    def columns(side, chunk):
        return pl.ds(pl.multiple_of(side * half + chunk * width, width), width)

    def send_to(seq, src, dst, send_sem, recv_sem):
        pltpu.make_async_remote_copy(
            src_ref=src, dst_ref=dst, send_sem=send_sem, recv_sem=recv_sem,
            device_id={"seq": seq}, device_id_type=mesh_id,
        ).start()

    for off in range(1, tps):
        other = lax.rem(mine + off, tps)
        pltpu.make_async_remote_copy(
            src_ref=hist.at[other], dst_ref=hist_tp.at[mine],
            send_sem=tp_send.at[off], recv_sem=tp_recv.at[mine],
            device_id={"tp": other}, device_id_type=mesh_id,
        ).start()
    pltpu.make_async_copy(hist.at[mine], hist_tp.at[mine], tp_recv.at[mine]).start()

    def send_far(chunk):
        @pl.when(z == 0)
        def _():
            for side in range(2):
                for kind, ref in enumerate((k_ref, v_ref)):
                    send_to(
                        2 + side, ref.at[:, columns(side, chunk)], far_kv.at[kind, y, chunk],
                        far_send.at[kind, side, chunk], far_kv_recv.at[kind, y, chunk],
                    )

        @pl.when(z == 2)
        def _():
            for side in range(2):
                send_to(
                    2 + side, q_ref.at[:, columns(side, chunk)], far_q.at[0, y, chunk],
                    far_send.at[0, side, chunk], far_q_recv.at[0, y, chunk],
                )

        @pl.when(z == 3)
        def _():
            for target in range(2):
                for side in range(2):
                    send_to(
                        2 + 2 * target + side, q_ref.at[:, columns(side, chunk)],
                        far_q.at[1, y, chunk],
                        far_send.at[target, side, chunk], far_q_recv.at[1, y, chunk],
                    )

    def send_own(chunk):
        for kind, ref in enumerate((q_ref, k_ref, v_ref)):
            send_to(
                peer, ref.at[:, columns(1 - y, chunk)], own.at[kind, y, chunk],
                own_send.at[kind, chunk], own_recv.at[kind, y, chunk],
            )
            pltpu.make_async_copy(
                ref.at[:, columns(y, chunk)], own.at[kind, y, chunk], own_recv.at[kind, y, chunk]
            ).start()

    send_far(0)
    send_own(0)
    for part in range(tps):
        wait(hist_tp.at[part], tp_recv.at[part])
    away = hist_tp.at[:, :, pl.ds(pl.multiple_of((1 - y) * half, half), half)]
    here = hist_tp.at[:, :, pl.ds(pl.multiple_of(y * half, half), half)]
    send_to(peer, away, slab.at[z, y], hy_send.at[0], hy_recv.at[y])
    pltpu.make_async_copy(here, slab.at[z, y], hy_recv.at[y]).start()
    for chunk in range(1, AHEAD):
        send_far(chunk)
        send_own(chunk)
    for side in range(2):
        wait(slab.at[z, side], hy_recv.at[side])

    def pass_slab(number, target):
        send_to(
            target * 2 + y, slab.at[number], slab.at[number], hz_send.at[number], hz_recv.at[number]
        )

    for origin in range(zs):
        pl.when(z == origin)(
            functools.partial(pass_slab, origin, 1 if origin == 0 else origin - 1)
        )

    @pl.when(z == 2)
    def _():
        wait(slab.at[3], hz_recv.at[3])
        pass_slab(3, 1)

    def advance(chunk):
        for kind in range(3):
            wait(own.at[kind, 0, chunk], own_send.at[kind, chunk])
        for origin, targets in ((0, 2), (2, 1), (3, 2)):

            @pl.when(z == origin)
            def _():
                for target in range(targets):
                    for side in range(2):
                        wait(far_q.at[0, 0, 0], far_send.at[target, side, chunk])

        @pl.when(chunk + AHEAD < CHUNKS)
        def _():
            send_far(chunk + AHEAD)
            send_own(chunk + AHEAD)

    def settle(number):
        past_rows = slab.shape[3] // 2
        count = 2 * tps * past_rows
        at = slice(number * count, (number + 1) * count)
        for chunk in range(CHUNKS):
            cut = slice(chunk * width, (chunk + 1) * width)
            blocks = [
                slab[number, side, part, :, cut].astype(jnp.float32)
                for side in range(2)
                for part in range(tps)
            ]
            past_k[chunk, at] = jnp.concatenate([b[:past_rows] for b in blocks], 0).astype(jnp.bfloat16)
            past_v[chunk, at] = jnp.concatenate([b[past_rows:] for b in blocks], 0).astype(jnp.bfloat16)

    def lanes(head):
        return slice(head * HEAD, (head + 1) * HEAD)

    def own_of(kind, chunk, head):
        return own[kind, :, chunk, :, lanes(head)].reshape(2 * rows, HEAD)

    def far_q_of(slot, chunk, head):
        return far_q[slot, :, chunk, :, lanes(head)].reshape(2 * rows, HEAD)

    def near_pair(chunk, head):
        return own_of(1, chunk, head), own_of(2, chunk, head)

    def far_pair(chunk, head):
        return tuple(
            far_kv[kind, :, chunk, :, lanes(head)].reshape(2 * rows, HEAD) for kind in range(2)
        )

    def past_pair(chunk, head, first, last):
        at = slice(first * past_k.shape[1] // zs, last * past_k.shape[1] // zs)
        return past_k[chunk, at, lanes(head)], past_v[chunk, at, lanes(head)]

    def wait_own(chunk):
        for kind in range(3):
            for side in range(2):
                wait(own.at[kind, side, chunk], own_recv.at[kind, side, chunk])

    def wait_far_q(slot, chunk):
        for side in range(2):
            wait(far_q.at[slot, side, chunk], far_q_recv.at[slot, side, chunk])

    def give(slot, target, source, chunk):
        send_to(
            target * 2 + y, give_o.at[slot, chunk], got_o.at[source, chunk],
            go_send.at[slot, chunk], go_recv.at[source, chunk],
        )
        send_to(
            target * 2 + y, give_l.at[slot, chunk], got_l.at[source, chunk],
            gl_send.at[slot, chunk], gl_recv.at[source, chunk],
        )

    def put_part(slot, chunk, head, part):
        give_o[slot, chunk, head] = part[0].astype(jnp.bfloat16)
        give_l[slot, chunk, head] = jnp.broadcast_to(part[1], give_l.shape[3:])

    def put_result(chunk, head, result):
        flat = jnp.transpose(result).astype(jnp.bfloat16)
        for side in range(2):
            o_buf[chunk, side, :, lanes(head)] = flat[side * rows : (side + 1) * rows]

    def finish_chunk(chunk):
        spot = o_ref.at[:, columns(y, chunk)]
        send_to(peer, o_buf.at[chunk, 1 - y], spot, fin_send.at[chunk], fin_recv.at[y, chunk])
        pltpu.make_async_copy(o_buf.at[chunk, y], spot, fin_recv.at[y, chunk]).start()

    def each_chunk(first, body):
        def step(chunk, unused):
            body(chunk)
            return unused

        lax.fori_loop(first, CHUNKS, step, 0)

    def wait_slabs(numbers):
        for number in numbers:
            wait(slab.at[number], hz_recv.at[number])

    def sent_slabs(numbers):
        for number in numbers:
            wait(slab.at[number], hz_send.at[number])

    def sent_parts(slots):
        def body(chunk):
            for slot in slots:
                wait(give_o.at[slot, chunk], go_send.at[slot, chunk])
                wait(give_l.at[slot, chunk], gl_send.at[slot, chunk])

        each_chunk(0, body)

    @pl.when(z == 0)
    def _():
        each_chunk(0, advance)
        wait_slabs((1, 2, 3))
        for number in range(zs):
            settle(number)

        def body(chunk):
            wait_own(chunk)
            for head in range(heads):
                pieces = [past_pair(chunk, head, 0, zs), near_pair(chunk, head)]
                put_result(chunk, head, partial(own_of(0, chunk, head), pieces, True)[0])
            finish_chunk(chunk)

        each_chunk(0, body)
        sent_slabs((0,))

    @pl.when(z == 1)
    def _():
        wait_slabs((0,))
        settle(0)
        settle(1)

        def far_part(chunk):
            advance(chunk)
            wait_own(chunk)
            for kind in range(2):
                for side in range(2):
                    wait(far_kv.at[kind, side, chunk], far_kv_recv.at[kind, side, chunk])
            for slot in (1, 0):
                wait_far_q(slot, chunk)
                for head in range(heads):
                    pieces = [
                        past_pair(chunk, head, 0, 2), far_pair(chunk, head), near_pair(chunk, head)
                    ]
                    put_part(slot, chunk, head, partial(far_q_of(slot, chunk, head), pieces, False))
                give(slot, 2 + slot, 0, chunk)

        def own_part(chunk):
            for head in range(heads):
                pieces = [
                    past_pair(chunk, head, 0, zs), far_pair(chunk, head), near_pair(chunk, head)
                ]
                put_result(chunk, head, partial(own_of(0, chunk, head), pieces, True)[0])
            finish_chunk(chunk)

        def body(chunk):
            far_part(chunk)

            @pl.when(chunk == 0)
            def _():
                for number in (2, 3):
                    wait_slabs((number,))
                    pass_slab(number, 0)
                    settle(number)

            own_part(chunk)

        each_chunk(0, body)
        sent_slabs((1, 2, 3))
        sent_parts((0, 1))

    def keep(chunk, head, part):
        keep_o[chunk, head] = part[0]
        keep_l[chunk, head] = jnp.broadcast_to(part[1], keep_l.shape[2:])

    def combine(sources):
        def body(chunk):
            for source in sources:
                wait(got_o.at[source, chunk], go_recv.at[source, chunk])
                wait(got_l.at[source, chunk], gl_recv.at[source, chunk])
            for head in range(heads):
                parts = [(keep_o[chunk, head], keep_l[chunk, head, :1])]
                for source in sources:
                    parts.append(
                        (
                            got_o[source, chunk, head].astype(jnp.float32),
                            got_l[source, chunk, head, :1],
                        )
                    )
                put_result(chunk, head, merge(parts))
            finish_chunk(chunk)

        each_chunk(0, body)

    @pl.when(z == 2)
    def _():
        settle(2)
        settle(3)

        def body(chunk):
            advance(chunk)
            wait_own(chunk)
            wait_far_q(1, chunk)
            for head in range(heads):
                pieces = [past_pair(chunk, head, 2, zs), near_pair(chunk, head)]
                put_part(1, chunk, head, partial(far_q_of(1, chunk, head), pieces, False))
            give(1, 3, 1, chunk)
            for head in range(heads):
                pieces = [past_pair(chunk, head, 2, zs), near_pair(chunk, head)]
                keep(chunk, head, partial(own_of(0, chunk, head), pieces, True))

        each_chunk(0, body)
        combine((0,))
        sent_slabs((2, 3))
        sent_parts((1,))

    @pl.when(z == 3)
    def _():
        def body(chunk):
            advance(chunk)
            wait_own(chunk)
            for head in range(heads):
                keep(chunk, head, partial(own_of(0, chunk, head), [near_pair(chunk, head)], True))

        each_chunk(0, body)
        combine((0, 1))
        sent_slabs((3,))

    for off in range(1, tps):
        wait(hist.at[0], tp_send.at[off])
    wait(slab.at[0, 0], hy_send.at[0])

    def last(chunk):
        wait(o_buf.at[chunk, 0], fin_send.at[chunk])
        for side in range(2):
            wait(o_ref.at[:, columns(side, chunk)], fin_recv.at[side, chunk])

    each_chunk(0, last)


def local_chain(tps, att_query, att_key, att_value, past_key, past_value):
    rows, wide = att_query.shape
    half = wide // 2
    width = half // CHUNKS
    heads = width // HEAD
    past_rows = past_key.shape[0]
    depth = past_rows * 8 * tps
    far = pl.BlockSpec(memory_space=pltpu.HBM)
    near = pl.BlockSpec(memory_space=pltpu.VMEM)
    dma = pltpu.SemaphoreType.DMA

    def held(*shape):
        return pltpu.VMEM(shape, jnp.bfloat16)

    def wider(*shape):
        return pltpu.VMEM(shape, jnp.float32)

    return pl.pallas_call(
        functools.partial(chain_kernel, tps),
        out_shape=jax.ShapeDtypeStruct((rows, wide), jnp.bfloat16),
        in_specs=[far, far, far, near, near],
        out_specs=near,
        scratch_shapes=[
            held(tps, 2 * past_rows, wide),
            held(tps, 2 * past_rows, wide),
            held(4, 2, tps, 2 * past_rows, half),
            held(CHUNKS, depth, width),
            held(CHUNKS, depth, width),
            held(3, 2, CHUNKS, rows, width),
            held(2, 2, CHUNKS, rows, width),
            held(2, 2, CHUNKS, rows, width),
            held(2, CHUNKS, heads, HEAD, 2 * rows),
            wider(2, CHUNKS, heads, 8, 2 * rows),
            held(2, CHUNKS, heads, HEAD, 2 * rows),
            wider(2, CHUNKS, heads, 8, 2 * rows),
            wider(CHUNKS, heads, HEAD, 2 * rows),
            wider(CHUNKS, heads, 8, 2 * rows),
            held(CHUNKS, 2, rows, width),
            dma((tps,)),
            dma((tps,)),
            dma((1,)),
            dma((2,)),
            dma((4,)),
            dma((4,)),
            dma((3, CHUNKS)),
            dma((3, 2, CHUNKS)),
            dma((2, 2, CHUNKS)),
            dma((2, 2, CHUNKS)),
            dma((2, 2, CHUNKS)),
            dma((2, CHUNKS)),
            dma((2, CHUNKS)),
            dma((2, CHUNKS)),
            dma((2, CHUNKS)),
            dma((CHUNKS,)),
            dma((2, CHUNKS)),
        ],
        compiler_params=pltpu.CompilerParams(
            collective_id=0, has_side_effects=True, vmem_limit_bytes=40 * 2**20
        ),
    )(att_query, att_key, att_value, past_key, past_value)


def local(att_query, att_key, att_value, past_key, past_value):
    seqs, tps = lax.axis_size("seq"), lax.axis_size("tp")
    rows, wide = att_query.shape
    fits = wide % (2 * CHUNKS * HEAD) == 0 and wide * tps == past_key.shape[1]
    if seqs == 8 and fits and past_key.shape[0] == 8 and rows == 128:
        return local_chain(tps, att_query, att_key, att_value, past_key, past_value)
    return local_xla(att_query, att_key, att_value, past_key, past_value)


def solution(mesh):
    placed = (
        P("seq", "tp"),
        P("seq", "tp"),
        P("seq", "tp"),
        P(("seq", "tp"), None),
        P(("seq", "tp"), None),
    )
    return jax.shard_map(
        local, mesh=mesh, in_specs=placed, out_specs=P("seq", "tp"), check_vma=False
    )
```

```python
import functools

import jax
import jax.numpy as jnp
from jax import lax
from jax.experimental import pallas as pl
from jax.experimental.pallas import tpu as pltpu
from jax.sharding import PartitionSpec as P

HEAD = 128


NEGATIVE = -1e30


def split_heads(block):
    return block.reshape(block.shape[0], block.shape[1] // HEAD, HEAD)


def absorb(state, queries, query_pos, keys, values, key_pos):
    maxima, totals, sums = state
    scores = jnp.einsum(
        "hqd,khd->hqk", queries, keys, preferred_element_type=jnp.float32
    ) * HEAD ** (-0.5)
    allowed = key_pos[None, None, :] <= query_pos[None, :, None]
    scores = jnp.where(allowed, scores, NEGATIVE)
    newmax = jnp.maximum(maxima, jnp.max(scores, axis=2))
    factor = jnp.exp(maxima - newmax)
    weights = jnp.where(allowed, jnp.exp(scores - newmax[:, :, None]), 0.0)
    totals = totals * factor + jnp.sum(weights, axis=2)
    sums = sums * factor[:, :, None] + jnp.einsum(
        "hqk,khd->hqd", weights.astype(jnp.bfloat16), values, preferred_element_type=jnp.float32
    )
    return (newmax, totals, sums)


def absorb_when_needed(state, queries, query_pos, keys, values, key_pos):
    return lax.cond(
        jnp.min(key_pos) > jnp.max(query_pos),
        lambda carried: carried,
        lambda carried: absorb(carried, queries, query_pos, keys, values, key_pos),
        state,
    )


def finish(state):
    maxima, totals, sums = state
    result = sums / totals[:, :, None]
    return jnp.transpose(result, (1, 0, 2)).reshape(result.shape[1], -1).astype(jnp.bfloat16)


def empty_state(head_count, count):
    return (
        jnp.full((head_count, count), NEGATIVE, jnp.float32),
        jnp.zeros((head_count, count), jnp.float32),
        jnp.zeros((head_count, count, HEAD), jnp.float32),
    )


def local_xla(att_query, att_key, att_value, past_key, past_value):
    seq_count = lax.axis_size("seq")
    position = lax.axis_index("seq")
    past_keys, past_values = (
        lax.all_to_all(past_key, "tp", split_axis=1, concat_axis=0, tiled=True),
        lax.all_to_all(past_value, "tp", split_axis=1, concat_axis=0, tiled=True),
    )
    past_rows = past_keys.shape[0]
    hist_total = past_rows * seq_count
    rows = att_query.shape[0]
    heads_here = att_query.shape[1] // HEAD
    per_device = max(1, heads_here // seq_count)
    repeat = max(1, seq_count // heads_here)
    span = past_rows + rows

    def spread(block):
        return jnp.tile(split_heads(block), (1, repeat, 1))

    stacked_keys = jnp.concatenate([past_keys, att_key], 0)
    stacked_values = jnp.concatenate([past_values, att_value], 0)
    got_query, got_keys, got_values = (
        lax.all_to_all(spread(att_query), "seq", split_axis=1, concat_axis=0, tiled=True),
        lax.all_to_all(spread(stacked_keys), "seq", split_axis=1, concat_axis=0, tiled=True),
        lax.all_to_all(spread(stacked_values), "seq", split_axis=1, concat_axis=0, tiled=True),
    )
    stretch_total = rows * seq_count
    copy_index = position // heads_here
    piece = stretch_total // (2 * repeat)
    first_start = copy_index * piece
    second_start = (2 * repeat - 1 - copy_index) * piece
    offsets = jnp.arange(piece, dtype=jnp.int32)
    pos_one = hist_total + first_start + offsets
    pos_two = hist_total + second_start + offsets
    query_one = jnp.transpose(lax.dynamic_slice_in_dim(got_query, first_start, piece, 0), (1, 0, 2))
    query_two = jnp.transpose(
        lax.dynamic_slice_in_dim(got_query, second_start, piece, 0), (1, 0, 2)
    )
    source = jnp.arange(seq_count, dtype=jnp.int32)[:, None]
    within = jnp.arange(span, dtype=jnp.int32)[None, :]
    key_table = jnp.where(
        within < past_rows,
        source * past_rows + within,
        hist_total + source * rows + within - past_rows,
    )
    turns = seq_count // 2
    key_blocks = got_keys.reshape(turns, 2 * span, per_device, HEAD)
    value_blocks = got_values.reshape(turns, 2 * span, per_device, HEAD)
    pos_blocks = key_table.reshape(turns, 2 * span)

    def step_block(carry_now, items):
        keys, values, key_pos = items
        return (
            (
                absorb_when_needed(carry_now[0], query_one, pos_one, keys, values, key_pos),
                absorb_when_needed(carry_now[1], query_two, pos_two, keys, values, key_pos),
            ),
            None,
        )

    start_state = empty_state(per_device, piece)
    carry, unused = lax.scan(
        step_block, (start_state, start_state), (key_blocks, value_blocks, pos_blocks)
    )
    placed = jnp.zeros((stretch_total, per_device * HEAD), jnp.bfloat16)
    placed = lax.dynamic_update_slice_in_dim(placed, finish(carry[0]), first_start, 0)
    placed = lax.dynamic_update_slice_in_dim(placed, finish(carry[1]), second_start, 0)
    returned = lax.all_to_all(
        placed.reshape(stretch_total, per_device, HEAD),
        "seq",
        split_axis=0,
        concat_axis=1,
        tiled=True,
    )
    summed = jnp.sum(returned.reshape(rows, repeat, heads_here, HEAD).astype(jnp.float32), axis=1)
    return summed.reshape(rows, heads_here * HEAD).astype(jnp.bfloat16)


SCALE = HEAD ** (-0.5)
LOG2E = 1.4426950408889634
CHUNKS = 4
HEADWAY = 2


def partial(query, pieces, diagonal):
    contract = (((1,), (1,)), ((), ()))
    found = [
        lax.dot_general(keys, query, contract, preferred_element_type=jnp.float32)
        for keys, values in pieces
    ]
    if diagonal:
        shape = found[-1].shape
        key_at = lax.broadcasted_iota(jnp.int32, shape, 0)
        query_at = lax.broadcasted_iota(jnp.int32, shape, 1)
        found[-1] = jnp.where(key_at <= query_at, found[-1], NEGATIVE)
    highest = functools.reduce(
        jnp.maximum, [jnp.max(scores, axis=0, keepdims=True) for scores in found]
    )
    total = jnp.zeros_like(highest)
    summed = jnp.zeros((HEAD, query.shape[0]), jnp.float32)
    for scores, (keys, values) in zip(found, pieces):
        weights = jnp.exp2((scores - highest) * (SCALE * LOG2E))
        total += jnp.sum(weights, axis=0, keepdims=True)
        summed += lax.dot_general(
            values, weights.astype(jnp.bfloat16), (((0,), (0,)), ((), ())),
            preferred_element_type=jnp.float32,
        )
    return summed / total, highest * SCALE + jnp.log(total)


def merge(parts):
    top = functools.reduce(jnp.maximum, [level for rows, level in parts])
    shares = [jnp.exp(level - top) for rows, level in parts]
    out = sum(rows * share for (rows, level), share in zip(parts, shares))
    return out / sum(shares)


def wait(ref, sem):
    pltpu.make_async_copy(ref, ref, sem).wait()


def chain_kernel(
    tps, q_ref, k_ref, v_ref, pk_ref, pv_ref, o_ref,
    hist, hist_tp, slab, past_k, past_v, own, far_q, far_kv, got_o, got_l, give_o, give_l,
    keep_o, keep_l, o_buf,
    tp_send, tp_recv, hy_send, hy_recv, hz_send, hz_recv, own_send, own_recv,
    far_send, far_q_recv, far_kv_recv, go_send, go_recv, gl_send, gl_recv, fin_send, fin_recv,
):
    seqs, zs = 8, 4
    me = lax.axis_index("seq")
    mine = lax.axis_index("tp")
    z, y = me // 2, lax.rem(me, 2)
    peer = z * 2 + 1 - y
    rows, wide = q_ref.shape
    half = wide // 2
    width = half // CHUNKS
    heads = width // HEAD
    mesh_id = pl.DeviceIdType.MESH

    barrier = pltpu.get_barrier_semaphore()
    for off in range(1, seqs):
        pl.semaphore_signal(
            barrier, inc=1, device_id={"seq": lax.rem(me + off, seqs)}, device_id_type=mesh_id
        )
    for off in range(1, tps):
        pl.semaphore_signal(
            barrier, inc=1, device_id={"tp": lax.rem(mine + off, tps)}, device_id_type=mesh_id
        )
    for part in range(tps):
        at = slice(part * wide, (part + 1) * wide)
        both = [pk_ref[:, at].astype(jnp.float32), pv_ref[:, at].astype(jnp.float32)]
        hist[part] = jnp.concatenate(both, 0).astype(jnp.bfloat16)
    pl.semaphore_wait(barrier, seqs + tps - 2)

    def columns(side, chunk):
        return pl.ds(pl.multiple_of(side * half + chunk * width, width), width)

    def send_to(seq, src, dst, send_sem, recv_sem):
        pltpu.make_async_remote_copy(
            src_ref=src, dst_ref=dst, send_sem=send_sem, recv_sem=recv_sem,
            device_id={"seq": seq}, device_id_type=mesh_id,
        ).start()

    for off in range(1, tps):
        other = lax.rem(mine + off, tps)
        pltpu.make_async_remote_copy(
            src_ref=hist.at[other], dst_ref=hist_tp.at[mine],
            send_sem=tp_send.at[off], recv_sem=tp_recv.at[mine],
            device_id={"tp": other}, device_id_type=mesh_id,
        ).start()
    pltpu.make_async_copy(hist.at[mine], hist_tp.at[mine], tp_recv.at[mine]).start()

    def forward(chunk):
        for origin, kind, target, buf, slot, sem in (
            (0, 1, 1, far_kv, 0, far_kv_recv),
            (0, 2, 1, far_kv, 1, far_kv_recv),
            (2, 0, 1, far_q, 0, far_q_recv),
            (3, 0, 1, far_q, 1, far_q_recv),
            (3, 0, 2, far_q, 1, far_q_recv),
        ):
            number = slot if origin == 0 else 2 - target

            @pl.when(z == origin)
            def _():
                send_to(
                    target * 2 + y, own.at[kind, :, chunk], buf.at[slot, :, chunk],
                    far_send.at[number, chunk], sem.at[slot, chunk],
                )

    def send_own(kind, chunk):
        ref = (q_ref, k_ref, v_ref)[kind]
        send_to(
            peer, ref.at[:, columns(1 - y, chunk)], own.at[kind, y, chunk],
            own_send.at[kind, chunk], own_recv.at[kind, y, chunk],
        )
        pltpu.make_async_copy(
            ref.at[:, columns(y, chunk)], own.at[kind, y, chunk], own_recv.at[kind, y, chunk]
        ).start()

    def wait_own(kind, chunk):
        for side in range(2):
            wait(own.at[kind, side, chunk], own_recv.at[kind, side, chunk])

    @pl.when(z >= 2)
    def _():
        for chunk in range(CHUNKS):
            send_own(0, chunk)

    @pl.when(z < 2)
    def _():
        for chunk in range(CHUNKS):
            send_own(1, chunk)
            send_own(2, chunk)

    for part in range(tps):
        wait(hist_tp.at[part], tp_recv.at[part])
    away = hist_tp.at[:, :, pl.ds(pl.multiple_of((1 - y) * half, half), half)]
    here = hist_tp.at[:, :, pl.ds(pl.multiple_of(y * half, half), half)]
    send_to(peer, away, slab.at[z, y], hy_send.at[0], hy_recv.at[y])
    pltpu.make_async_copy(here, slab.at[z, y], hy_recv.at[y]).start()

    @pl.when(z >= 2)
    def _():
        for chunk in range(CHUNKS):
            send_own(1, chunk)
            send_own(2, chunk)
        for chunk in range(HEADWAY):
            wait_own(0, chunk)
            forward(chunk)

    @pl.when(z < 2)
    def _():
        for chunk in range(CHUNKS):
            send_own(0, chunk)

    for side in range(2):
        wait(slab.at[z, side], hy_recv.at[side])

    def pass_slab(number, target):
        send_to(
            target * 2 + y, slab.at[number], slab.at[number], hz_send.at[number], hz_recv.at[number]
        )

    for origin in range(zs):
        pl.when(z == origin)(
            functools.partial(pass_slab, origin, 1 if origin == 0 else origin - 1)
        )

    @pl.when(z == 2)
    def _():
        wait(slab.at[3], hz_recv.at[3])
        pass_slab(3, 1)

    @pl.when(z >= 2)
    def _():
        for chunk in range(HEADWAY, CHUNKS):
            wait_own(0, chunk)
            forward(chunk)

    @pl.when(z == 0)
    def _():
        for chunk in range(CHUNKS):
            wait_own(1, chunk)
            wait_own(2, chunk)
            forward(chunk)

    def settle(number):
        past_rows = slab.shape[3] // 2
        count = 2 * tps * past_rows
        at = slice(number * count, (number + 1) * count)
        for chunk in range(CHUNKS):
            cut = slice(chunk * width, (chunk + 1) * width)
            blocks = [
                slab[number, side, part, :, cut].astype(jnp.float32)
                for side in range(2)
                for part in range(tps)
            ]
            past_k[chunk, at] = jnp.concatenate([b[:past_rows] for b in blocks], 0).astype(jnp.bfloat16)
            past_v[chunk, at] = jnp.concatenate([b[past_rows:] for b in blocks], 0).astype(jnp.bfloat16)

    def lanes(head):
        return slice(head * HEAD, (head + 1) * HEAD)

    def own_of(kind, chunk, head):
        return own[kind, :, chunk, :, lanes(head)].reshape(2 * rows, HEAD)

    def far_q_of(slot, chunk, head):
        return far_q[slot, :, chunk, :, lanes(head)].reshape(2 * rows, HEAD)

    def near_pair(chunk, head):
        return own_of(1, chunk, head), own_of(2, chunk, head)

    def far_pair(chunk, head):
        return tuple(
            far_kv[kind, :, chunk, :, lanes(head)].reshape(2 * rows, HEAD) for kind in range(2)
        )

    def past_pair(chunk, head, first, last):
        at = slice(first * past_k.shape[1] // zs, last * past_k.shape[1] // zs)
        return past_k[chunk, at, lanes(head)], past_v[chunk, at, lanes(head)]

    def wait_far_q(slot, chunk):
        wait(far_q.at[slot, :, chunk], far_q_recv.at[slot, chunk])

    def give(slot, target, source, chunk):
        send_to(
            target * 2 + y, give_o.at[slot, chunk], got_o.at[source, chunk],
            go_send.at[slot, chunk], go_recv.at[source, chunk],
        )
        send_to(
            target * 2 + y, give_l.at[slot, chunk], got_l.at[source, chunk],
            gl_send.at[slot, chunk], gl_recv.at[source, chunk],
        )

    def put_part(slot, chunk, head, part):
        give_o[slot, chunk, head] = part[0].astype(jnp.bfloat16)
        give_l[slot, chunk, head] = jnp.broadcast_to(part[1], give_l.shape[3:])

    def put_result(chunk, head, result):
        flat = jnp.transpose(result).astype(jnp.bfloat16)
        for side in range(2):
            o_buf[chunk, side, :, lanes(head)] = flat[side * rows : (side + 1) * rows]

    def finish_chunk(chunk):
        spot = o_ref.at[:, columns(y, chunk)]
        send_to(peer, o_buf.at[chunk, 1 - y], spot, fin_send.at[chunk], fin_recv.at[y, chunk])
        pltpu.make_async_copy(o_buf.at[chunk, y], spot, fin_recv.at[y, chunk]).start()

    def each_chunk(first, body):
        def step(chunk, unused):
            body(chunk)
            return unused

        lax.fori_loop(first, CHUNKS, step, 0)

    def wait_slabs(numbers):
        for number in numbers:
            wait(slab.at[number], hz_recv.at[number])

    def sent_slabs(numbers):
        for number in numbers:
            wait(slab.at[number], hz_send.at[number])

    def sent_parts(slots):
        def body(chunk):
            for slot in slots:
                wait(give_o.at[slot, chunk], go_send.at[slot, chunk])
                wait(give_l.at[slot, chunk], gl_send.at[slot, chunk])

        each_chunk(0, body)

    @pl.when(z == 0)
    def _():
        wait_slabs((1, 2, 3))
        for number in range(zs):
            settle(number)

        def body(chunk):
            wait_own(0, chunk)
            for head in range(heads):
                pieces = [past_pair(chunk, head, 0, zs), near_pair(chunk, head)]
                put_result(chunk, head, partial(own_of(0, chunk, head), pieces, True)[0])
            finish_chunk(chunk)

        each_chunk(0, body)
        sent_slabs((0,))

    @pl.when(z == 1)
    def _():
        wait_slabs((0,))
        settle(0)
        settle(1)

        def far_part(chunk):
            for kind in range(3):
                wait_own(kind, chunk)
            for kind in range(2):
                wait(far_kv.at[kind, :, chunk], far_kv_recv.at[kind, chunk])
            for slot in (1, 0):
                wait_far_q(slot, chunk)
                for head in range(heads):
                    pieces = [
                        past_pair(chunk, head, 0, 2), far_pair(chunk, head), near_pair(chunk, head)
                    ]
                    put_part(slot, chunk, head, partial(far_q_of(slot, chunk, head), pieces, False))
                give(slot, 2 + slot, 0, chunk)

        def own_part(chunk):
            for head in range(heads):
                pieces = [
                    past_pair(chunk, head, 0, zs), far_pair(chunk, head), near_pair(chunk, head)
                ]
                put_result(chunk, head, partial(own_of(0, chunk, head), pieces, True)[0])
            finish_chunk(chunk)

        def body(chunk):
            far_part(chunk)

            @pl.when(chunk == 1)
            def _():
                for number in (2, 3):
                    wait_slabs((number,))
                    pass_slab(number, 0)
                    settle(number)

            @pl.when(chunk >= 1)
            def _():
                own_part(chunk - 1)

        each_chunk(0, body)
        own_part(CHUNKS - 1)
        sent_slabs((1, 2, 3))
        sent_parts((0, 1))

    def keep(chunk, head, part):
        keep_o[chunk, head] = part[0]
        keep_l[chunk, head] = jnp.broadcast_to(part[1], keep_l.shape[2:])

    def combine(sources):
        def body(chunk):
            for source in sources:
                wait(got_o.at[source, chunk], go_recv.at[source, chunk])
                wait(got_l.at[source, chunk], gl_recv.at[source, chunk])
            for head in range(heads):
                parts = [(keep_o[chunk, head], keep_l[chunk, head, :1])]
                for source in sources:
                    parts.append(
                        (
                            got_o[source, chunk, head].astype(jnp.float32),
                            got_l[source, chunk, head, :1],
                        )
                    )
                put_result(chunk, head, merge(parts))
            finish_chunk(chunk)

        each_chunk(0, body)

    @pl.when(z == 2)
    def _():
        settle(2)
        settle(3)

        def body(chunk):
            wait_own(1, chunk)
            wait_own(2, chunk)
            wait_far_q(1, chunk)
            for head in range(heads):
                pieces = [past_pair(chunk, head, 2, zs), near_pair(chunk, head)]
                put_part(1, chunk, head, partial(far_q_of(1, chunk, head), pieces, False))
            give(1, 3, 1, chunk)
            for head in range(heads):
                pieces = [past_pair(chunk, head, 2, zs), near_pair(chunk, head)]
                keep(chunk, head, partial(own_of(0, chunk, head), pieces, True))

        each_chunk(0, body)
        combine((0,))
        sent_slabs((2, 3))
        sent_parts((1,))

    @pl.when(z == 3)
    def _():
        def body(chunk):
            wait_own(1, chunk)
            wait_own(2, chunk)
            for head in range(heads):
                keep(chunk, head, partial(own_of(0, chunk, head), [near_pair(chunk, head)], True))

        each_chunk(0, body)
        combine((0, 1))
        sent_slabs((3,))

    for off in range(1, tps):
        wait(hist.at[0], tp_send.at[off])
    wait(slab.at[0, 0], hy_send.at[0])

    def last(chunk):
        for kind in range(3):
            wait(own.at[kind, 0, chunk], own_send.at[kind, chunk])
        for origin, targets in ((0, 2), (2, 1), (3, 2)):

            @pl.when(z == origin)
            def _():
                for target in range(targets):
                    wait(far_q.at[0, :, chunk], far_send.at[1 - target if origin == 2 else target, chunk])

        wait(o_buf.at[chunk, 0], fin_send.at[chunk])
        for side in range(2):
            wait(o_ref.at[:, columns(side, chunk)], fin_recv.at[side, chunk])

    each_chunk(0, last)


def local_chain(tps, att_query, att_key, att_value, past_key, past_value):
    rows, wide = att_query.shape
    half = wide // 2
    width = half // CHUNKS
    heads = width // HEAD
    past_rows = past_key.shape[0]
    depth = past_rows * 8 * tps
    far = pl.BlockSpec(memory_space=pltpu.HBM)
    near = pl.BlockSpec(memory_space=pltpu.VMEM)
    dma = pltpu.SemaphoreType.DMA

    def held(*shape):
        return pltpu.VMEM(shape, jnp.bfloat16)

    def wider(*shape):
        return pltpu.VMEM(shape, jnp.float32)

    return pl.pallas_call(
        functools.partial(chain_kernel, tps),
        out_shape=jax.ShapeDtypeStruct((rows, wide), jnp.bfloat16),
        in_specs=[far, far, far, near, near],
        out_specs=far,
        scratch_shapes=[
            held(tps, 2 * past_rows, wide),
            held(tps, 2 * past_rows, wide),
            held(4, 2, tps, 2 * past_rows, half),
            held(CHUNKS, depth, width),
            held(CHUNKS, depth, width),
            held(3, 2, CHUNKS, rows, width),
            held(2, 2, CHUNKS, rows, width),
            held(2, 2, CHUNKS, rows, width),
            held(2, CHUNKS, heads, HEAD, 2 * rows),
            wider(2, CHUNKS, heads, 8, 2 * rows),
            held(2, CHUNKS, heads, HEAD, 2 * rows),
            wider(2, CHUNKS, heads, 8, 2 * rows),
            wider(CHUNKS, heads, HEAD, 2 * rows),
            wider(CHUNKS, heads, 8, 2 * rows),
            held(CHUNKS, 2, rows, width),
            dma((tps,)),
            dma((tps,)),
            dma((1,)),
            dma((2,)),
            dma((4,)),
            dma((4,)),
            dma((3, CHUNKS)),
            dma((3, 2, CHUNKS)),
            dma((2, CHUNKS)),
            dma((2, CHUNKS)),
            dma((2, CHUNKS)),
            dma((2, CHUNKS)),
            dma((2, CHUNKS)),
            dma((2, CHUNKS)),
            dma((2, CHUNKS)),
            dma((CHUNKS,)),
            dma((2, CHUNKS)),
        ],
        compiler_params=pltpu.CompilerParams(
            collective_id=0, has_side_effects=True, vmem_limit_bytes=56 * 2**20
        ),
    )(att_query, att_key, att_value, past_key, past_value)


def local(att_query, att_key, att_value, past_key, past_value):
    seqs, tps = lax.axis_size("seq"), lax.axis_size("tp")
    rows, wide = att_query.shape
    fits = wide % (2 * CHUNKS * HEAD) == 0 and wide * tps == past_key.shape[1]
    if seqs == 8 and fits and past_key.shape[0] == 8 and rows == 128:
        return local_chain(tps, att_query, att_key, att_value, past_key, past_value)
    return local_xla(att_query, att_key, att_value, past_key, past_value)


def solution(mesh):
    placed = (
        P("seq", "tp"),
        P("seq", "tp"),
        P("seq", "tp"),
        P(("seq", "tp"), None),
        P(("seq", "tp"), None),
    )
    return jax.shard_map(
        local, mesh=mesh, in_specs=placed, out_specs=P("seq", "tp"), check_vma=False
    )
```

```python
import functools

import jax
import jax.numpy as jnp
from jax import lax
from jax.experimental import pallas as pl
from jax.experimental.pallas import tpu as pltpu
from jax.sharding import PartitionSpec as P

HEAD = 128


NEGATIVE = -1e30


def split_heads(block):
    return block.reshape(block.shape[0], block.shape[1] // HEAD, HEAD)


def absorb(state, queries, query_pos, keys, values, key_pos):
    maxima, totals, sums = state
    scores = jnp.einsum(
        "hqd,khd->hqk", queries, keys, preferred_element_type=jnp.float32
    ) * HEAD ** (-0.5)
    allowed = key_pos[None, None, :] <= query_pos[None, :, None]
    scores = jnp.where(allowed, scores, NEGATIVE)
    newmax = jnp.maximum(maxima, jnp.max(scores, axis=2))
    factor = jnp.exp(maxima - newmax)
    weights = jnp.where(allowed, jnp.exp(scores - newmax[:, :, None]), 0.0)
    totals = totals * factor + jnp.sum(weights, axis=2)
    sums = sums * factor[:, :, None] + jnp.einsum(
        "hqk,khd->hqd", weights.astype(jnp.bfloat16), values, preferred_element_type=jnp.float32
    )
    return (newmax, totals, sums)


def absorb_when_needed(state, queries, query_pos, keys, values, key_pos):
    return lax.cond(
        jnp.min(key_pos) > jnp.max(query_pos),
        lambda carried: carried,
        lambda carried: absorb(carried, queries, query_pos, keys, values, key_pos),
        state,
    )


def finish(state):
    maxima, totals, sums = state
    result = sums / totals[:, :, None]
    return jnp.transpose(result, (1, 0, 2)).reshape(result.shape[1], -1).astype(jnp.bfloat16)


def empty_state(head_count, count):
    return (
        jnp.full((head_count, count), NEGATIVE, jnp.float32),
        jnp.zeros((head_count, count), jnp.float32),
        jnp.zeros((head_count, count, HEAD), jnp.float32),
    )


def local_xla(att_query, att_key, att_value, past_key, past_value):
    seq_count = lax.axis_size("seq")
    position = lax.axis_index("seq")
    past_keys, past_values = (
        lax.all_to_all(past_key, "tp", split_axis=1, concat_axis=0, tiled=True),
        lax.all_to_all(past_value, "tp", split_axis=1, concat_axis=0, tiled=True),
    )
    past_rows = past_keys.shape[0]
    hist_total = past_rows * seq_count
    rows = att_query.shape[0]
    heads_here = att_query.shape[1] // HEAD
    per_device = max(1, heads_here // seq_count)
    repeat = max(1, seq_count // heads_here)
    span = past_rows + rows

    def spread(block):
        return jnp.tile(split_heads(block), (1, repeat, 1))

    stacked_keys = jnp.concatenate([past_keys, att_key], 0)
    stacked_values = jnp.concatenate([past_values, att_value], 0)
    got_query, got_keys, got_values = (
        lax.all_to_all(spread(att_query), "seq", split_axis=1, concat_axis=0, tiled=True),
        lax.all_to_all(spread(stacked_keys), "seq", split_axis=1, concat_axis=0, tiled=True),
        lax.all_to_all(spread(stacked_values), "seq", split_axis=1, concat_axis=0, tiled=True),
    )
    stretch_total = rows * seq_count
    copy_index = position // heads_here
    piece = stretch_total // (2 * repeat)
    first_start = copy_index * piece
    second_start = (2 * repeat - 1 - copy_index) * piece
    offsets = jnp.arange(piece, dtype=jnp.int32)
    pos_one = hist_total + first_start + offsets
    pos_two = hist_total + second_start + offsets
    query_one = jnp.transpose(lax.dynamic_slice_in_dim(got_query, first_start, piece, 0), (1, 0, 2))
    query_two = jnp.transpose(
        lax.dynamic_slice_in_dim(got_query, second_start, piece, 0), (1, 0, 2)
    )
    source = jnp.arange(seq_count, dtype=jnp.int32)[:, None]
    within = jnp.arange(span, dtype=jnp.int32)[None, :]
    key_table = jnp.where(
        within < past_rows,
        source * past_rows + within,
        hist_total + source * rows + within - past_rows,
    )
    turns = seq_count // 2
    key_blocks = got_keys.reshape(turns, 2 * span, per_device, HEAD)
    value_blocks = got_values.reshape(turns, 2 * span, per_device, HEAD)
    pos_blocks = key_table.reshape(turns, 2 * span)

    def step_block(carry_now, items):
        keys, values, key_pos = items
        return (
            (
                absorb_when_needed(carry_now[0], query_one, pos_one, keys, values, key_pos),
                absorb_when_needed(carry_now[1], query_two, pos_two, keys, values, key_pos),
            ),
            None,
        )

    start_state = empty_state(per_device, piece)
    carry, unused = lax.scan(
        step_block, (start_state, start_state), (key_blocks, value_blocks, pos_blocks)
    )
    placed = jnp.zeros((stretch_total, per_device * HEAD), jnp.bfloat16)
    placed = lax.dynamic_update_slice_in_dim(placed, finish(carry[0]), first_start, 0)
    placed = lax.dynamic_update_slice_in_dim(placed, finish(carry[1]), second_start, 0)
    returned = lax.all_to_all(
        placed.reshape(stretch_total, per_device, HEAD),
        "seq",
        split_axis=0,
        concat_axis=1,
        tiled=True,
    )
    summed = jnp.sum(returned.reshape(rows, repeat, heads_here, HEAD).astype(jnp.float32), axis=1)
    return summed.reshape(rows, heads_here * HEAD).astype(jnp.bfloat16)


SCALE = HEAD ** (-0.5)
LOG2E = 1.4426950408889634
CHUNKS = 4
HEADWAY = 1


def partial(query, pieces, diagonal):
    contract = (((1,), (1,)), ((), ()))
    found = [
        lax.dot_general(keys, query, contract, preferred_element_type=jnp.float32)
        for keys, values in pieces
    ]
    if diagonal:
        shape = found[-1].shape
        key_at = lax.broadcasted_iota(jnp.int32, shape, 0)
        query_at = lax.broadcasted_iota(jnp.int32, shape, 1)
        found[-1] = jnp.where(key_at <= query_at, found[-1], NEGATIVE)
    highest = functools.reduce(
        jnp.maximum, [jnp.max(scores, axis=0, keepdims=True) for scores in found]
    )
    total = jnp.zeros_like(highest)
    summed = jnp.zeros((HEAD, query.shape[0]), jnp.float32)
    for scores, (keys, values) in zip(found, pieces):
        weights = jnp.exp2((scores - highest) * (SCALE * LOG2E))
        total += jnp.sum(weights, axis=0, keepdims=True)
        summed += lax.dot_general(
            values, weights.astype(jnp.bfloat16), (((0,), (0,)), ((), ())),
            preferred_element_type=jnp.float32,
        )
    return summed / total, highest * SCALE + jnp.log(total)


def merge(parts):
    top = functools.reduce(jnp.maximum, [level for rows, level in parts])
    shares = [jnp.exp(level - top) for rows, level in parts]
    out = sum(rows * share for (rows, level), share in zip(parts, shares))
    return out / sum(shares)


def wait(ref, sem):
    pltpu.make_async_copy(ref, ref, sem).wait()


def chain_kernel(
    tps, q_ref, k_ref, v_ref, pk_ref, pv_ref, o_ref,
    hist, hist_tp, slab, past_k, past_v, own, far_q, far_kv, got_o, got_l, give_o, give_l,
    keep_o, keep_l, o_buf,
    tp_send, tp_recv, hy_send, hy_recv, hz_send, hz_recv, own_send, own_recv,
    far_send, far_q_recv, far_kv_recv, go_send, go_recv, gl_send, gl_recv, fin_send, fin_recv,
):
    seqs, zs = 8, 4
    me = lax.axis_index("seq")
    mine = lax.axis_index("tp")
    z, y = me // 2, lax.rem(me, 2)
    peer = z * 2 + 1 - y
    rows, wide = q_ref.shape
    half = wide // 2
    width = half // CHUNKS
    heads = width // HEAD
    mesh_id = pl.DeviceIdType.MESH

    barrier = pltpu.get_barrier_semaphore()
    for off in range(1, seqs):
        pl.semaphore_signal(
            barrier, inc=1, device_id={"seq": lax.rem(me + off, seqs)}, device_id_type=mesh_id
        )
    for off in range(1, tps):
        pl.semaphore_signal(
            barrier, inc=1, device_id={"tp": lax.rem(mine + off, tps)}, device_id_type=mesh_id
        )
    for part in range(tps):
        at = slice(part * wide, (part + 1) * wide)
        both = [pk_ref[:, at].astype(jnp.float32), pv_ref[:, at].astype(jnp.float32)]
        hist[part] = jnp.concatenate(both, 0).astype(jnp.bfloat16)
    pl.semaphore_wait(barrier, seqs + tps - 2)

    def columns(side, chunk):
        return pl.ds(pl.multiple_of(side * half + chunk * width, width), width)

    def send_to(seq, src, dst, send_sem, recv_sem):
        pltpu.make_async_remote_copy(
            src_ref=src, dst_ref=dst, send_sem=send_sem, recv_sem=recv_sem,
            device_id={"seq": seq}, device_id_type=mesh_id,
        ).start()

    for off in range(1, tps):
        other = lax.rem(mine + off, tps)
        pltpu.make_async_remote_copy(
            src_ref=hist.at[other], dst_ref=hist_tp.at[mine],
            send_sem=tp_send.at[off], recv_sem=tp_recv.at[mine],
            device_id={"tp": other}, device_id_type=mesh_id,
        ).start()
    pltpu.make_async_copy(hist.at[mine], hist_tp.at[mine], tp_recv.at[mine]).start()

    def forward(chunk):
        for origin, kind, target, buf, slot, sem in (
            (0, 1, 1, far_kv, 0, far_kv_recv),
            (0, 2, 1, far_kv, 1, far_kv_recv),
            (2, 0, 1, far_q, 0, far_q_recv),
            (3, 0, 1, far_q, 1, far_q_recv),
            (3, 0, 2, far_q, 1, far_q_recv),
        ):
            number = slot if origin == 0 else 2 - target

            @pl.when(z == origin)
            def _():
                send_to(
                    target * 2 + y, own.at[kind, :, chunk], buf.at[slot, :, chunk],
                    far_send.at[number, chunk], sem.at[slot, chunk],
                )

    def send_own(kind, chunk):
        ref = (q_ref, k_ref, v_ref)[kind]
        send_to(
            peer, ref.at[:, columns(1 - y, chunk)], own.at[kind, y, chunk],
            own_send.at[kind, chunk], own_recv.at[kind, y, chunk],
        )
        pltpu.make_async_copy(
            ref.at[:, columns(y, chunk)], own.at[kind, y, chunk], own_recv.at[kind, y, chunk]
        ).start()

    def wait_own(kind, chunk):
        for side in range(2):
            wait(own.at[kind, side, chunk], own_recv.at[kind, side, chunk])

    @pl.when(z >= 2)
    def _():
        for chunk in range(CHUNKS):
            send_own(0, chunk)

    @pl.when(z < 2)
    def _():
        for chunk in range(CHUNKS):
            send_own(1, chunk)
            send_own(2, chunk)

    for part in range(tps):
        wait(hist_tp.at[part], tp_recv.at[part])
    away = hist_tp.at[:, :, pl.ds(pl.multiple_of((1 - y) * half, half), half)]
    here = hist_tp.at[:, :, pl.ds(pl.multiple_of(y * half, half), half)]
    send_to(peer, away, slab.at[z, y], hy_send.at[0], hy_recv.at[y])
    pltpu.make_async_copy(here, slab.at[z, y], hy_recv.at[y]).start()

    @pl.when(z >= 2)
    def _():
        for chunk in range(CHUNKS):
            send_own(1, chunk)
            send_own(2, chunk)
        for chunk in range(HEADWAY):
            wait_own(0, chunk)
            forward(chunk)

    @pl.when(z < 2)
    def _():
        for chunk in range(CHUNKS):
            send_own(0, chunk)

    for side in range(2):
        wait(slab.at[z, side], hy_recv.at[side])

    def pass_slab(number, target):
        send_to(
            target * 2 + y, slab.at[number], slab.at[number], hz_send.at[number], hz_recv.at[number]
        )

    for origin in range(zs):
        pl.when(z == origin)(
            functools.partial(pass_slab, origin, 1 if origin == 0 else origin - 1)
        )

    @pl.when(z == 2)
    def _():
        wait(slab.at[3], hz_recv.at[3])
        pass_slab(3, 1)
        wait(slab.at[2], hz_send.at[2])

    @pl.when(z >= 2)
    def _():
        wait(slab.at[3], hz_send.at[3])

    @pl.when(z >= 2)
    def _():
        for chunk in range(HEADWAY, CHUNKS):
            wait_own(0, chunk)
            forward(chunk)

    @pl.when(z == 0)
    def _():
        for chunk in range(CHUNKS):
            wait_own(1, chunk)
            wait_own(2, chunk)
            forward(chunk)

    def settle(number):
        past_rows = slab.shape[3] // 2
        count = 2 * tps * past_rows
        at = slice(number * count, (number + 1) * count)
        for chunk in range(CHUNKS):
            cut = slice(chunk * width, (chunk + 1) * width)
            blocks = [
                slab[number, side, part, :, cut].astype(jnp.float32)
                for side in range(2)
                for part in range(tps)
            ]
            past_k[chunk, at] = jnp.concatenate([b[:past_rows] for b in blocks], 0).astype(jnp.bfloat16)
            past_v[chunk, at] = jnp.concatenate([b[past_rows:] for b in blocks], 0).astype(jnp.bfloat16)

    def lanes(head):
        return slice(head * HEAD, (head + 1) * HEAD)

    def own_of(kind, chunk, head):
        return own[kind, :, chunk, :, lanes(head)].reshape(2 * rows, HEAD)

    def far_q_of(slot, chunk, head):
        return far_q[slot, :, chunk, :, lanes(head)].reshape(2 * rows, HEAD)

    def near_pair(chunk, head):
        return own_of(1, chunk, head), own_of(2, chunk, head)

    def far_pair(chunk, head):
        return tuple(
            far_kv[kind, :, chunk, :, lanes(head)].reshape(2 * rows, HEAD) for kind in range(2)
        )

    def past_pair(chunk, head, first, last):
        at = slice(first * past_k.shape[1] // zs, last * past_k.shape[1] // zs)
        return past_k[chunk, at, lanes(head)], past_v[chunk, at, lanes(head)]

    def wait_far_q(slot, chunk):
        wait(far_q.at[slot, :, chunk], far_q_recv.at[slot, chunk])

    def give(slot, target, source, chunk):
        send_to(
            target * 2 + y, give_o.at[slot, chunk], got_o.at[source, chunk],
            go_send.at[slot, chunk], go_recv.at[source, chunk],
        )
        send_to(
            target * 2 + y, give_l.at[slot, chunk], got_l.at[source, chunk],
            gl_send.at[slot, chunk], gl_recv.at[source, chunk],
        )

    def put_part(slot, chunk, head, part):
        give_o[slot, chunk, head] = part[0].astype(jnp.bfloat16)
        give_l[slot, chunk, head] = jnp.broadcast_to(part[1], give_l.shape[3:])

    def put_result(chunk, head, result):
        flat = jnp.transpose(result).astype(jnp.bfloat16)
        for side in range(2):
            o_buf[chunk, side, :, lanes(head)] = flat[side * rows : (side + 1) * rows]

    def finish_chunk(chunk):
        spot = o_ref.at[:, columns(y, chunk)]
        send_to(peer, o_buf.at[chunk, 1 - y], spot, fin_send.at[chunk], fin_recv.at[y, chunk])
        pltpu.make_async_copy(o_buf.at[chunk, y], spot, fin_recv.at[y, chunk]).start()

    def each_chunk(first, body):
        def step(chunk, unused):
            body(chunk)
            return unused

        lax.fori_loop(first, CHUNKS, step, 0)

    def wait_slabs(numbers):
        for number in numbers:
            wait(slab.at[number], hz_recv.at[number])

    def sent_slabs(numbers):
        for number in numbers:
            wait(slab.at[number], hz_send.at[number])

    def sent_parts(slots):
        def body(chunk):
            for slot in slots:
                wait(give_o.at[slot, chunk], go_send.at[slot, chunk])
                wait(give_l.at[slot, chunk], gl_send.at[slot, chunk])

        each_chunk(0, body)

    @pl.when(z == 0)
    def _():
        wait_slabs((1, 2, 3))
        for number in range(zs):
            settle(number)

        def body(chunk):
            wait_own(0, chunk)
            for head in range(heads):
                pieces = [past_pair(chunk, head, 0, zs), near_pair(chunk, head)]
                put_result(chunk, head, partial(own_of(0, chunk, head), pieces, True)[0])
            finish_chunk(chunk)

        each_chunk(0, body)
        sent_slabs((0,))

    @pl.when(z == 1)
    def _():
        wait_slabs((0,))
        settle(0)
        settle(1)

        def far_part(chunk):
            for kind in range(3):
                wait_own(kind, chunk)
            for kind in range(2):
                wait(far_kv.at[kind, :, chunk], far_kv_recv.at[kind, chunk])
            for slot in (1, 0):
                wait_far_q(slot, chunk)
                for head in range(heads):
                    pieces = [
                        past_pair(chunk, head, 0, 2), far_pair(chunk, head), near_pair(chunk, head)
                    ]
                    put_part(slot, chunk, head, partial(far_q_of(slot, chunk, head), pieces, False))
                give(slot, 2 + slot, 0, chunk)

        def own_part(chunk):
            for head in range(heads):
                pieces = [
                    past_pair(chunk, head, 0, zs), far_pair(chunk, head), near_pair(chunk, head)
                ]
                put_result(chunk, head, partial(own_of(0, chunk, head), pieces, True)[0])
            finish_chunk(chunk)

        def body(chunk):
            far_part(chunk)

            @pl.when(chunk == 0)
            def _():
                for number in (2, 3):
                    wait_slabs((number,))
                    pass_slab(number, 0)
                    settle(number)

            own_part(chunk)

        each_chunk(0, body)
        sent_slabs((1, 2, 3))
        sent_parts((0, 1))

    def keep(chunk, head, part):
        keep_o[chunk, head] = part[0]
        keep_l[chunk, head] = jnp.broadcast_to(part[1], keep_l.shape[2:])

    def combine(sources):
        def body(chunk):
            for source in sources:
                wait(got_o.at[source, chunk], go_recv.at[source, chunk])
                wait(got_l.at[source, chunk], gl_recv.at[source, chunk])
            for head in range(heads):
                parts = [(keep_o[chunk, head], keep_l[chunk, head, :1])]
                for source in sources:
                    parts.append(
                        (
                            got_o[source, chunk, head].astype(jnp.float32),
                            got_l[source, chunk, head, :1],
                        )
                    )
                put_result(chunk, head, merge(parts))
            finish_chunk(chunk)

        each_chunk(0, body)

    @pl.when(z == 2)
    def _():
        settle(2)
        settle(3)

        def body(chunk):
            wait_own(1, chunk)
            wait_own(2, chunk)
            wait_far_q(1, chunk)
            for head in range(heads):
                pieces = [past_pair(chunk, head, 2, zs), near_pair(chunk, head)]
                put_part(1, chunk, head, partial(far_q_of(1, chunk, head), pieces, False))
            give(1, 3, 1, chunk)
            for head in range(heads):
                pieces = [past_pair(chunk, head, 2, zs), near_pair(chunk, head)]
                keep(chunk, head, partial(own_of(0, chunk, head), pieces, True))

        each_chunk(0, body)
        combine((0,))
        sent_parts((1,))

    @pl.when(z == 3)
    def _():
        def body(chunk):
            wait_own(1, chunk)
            wait_own(2, chunk)
            for head in range(heads):
                keep(chunk, head, partial(own_of(0, chunk, head), [near_pair(chunk, head)], True))

        each_chunk(0, body)
        combine((0, 1))

    for off in range(1, tps):
        wait(hist.at[0], tp_send.at[off])
    wait(slab.at[0, 0], hy_send.at[0])

    def last(chunk):
        for kind in range(3):
            wait(own.at[kind, 0, chunk], own_send.at[kind, chunk])
        for origin, targets in ((0, 2), (2, 1), (3, 2)):

            @pl.when(z == origin)
            def _():
                for target in range(targets):
                    wait(far_q.at[0, :, chunk], far_send.at[1 - target if origin == 2 else target, chunk])

        wait(o_buf.at[chunk, 0], fin_send.at[chunk])
        for side in range(2):
            wait(o_ref.at[:, columns(side, chunk)], fin_recv.at[side, chunk])

    each_chunk(0, last)


def local_chain(tps, att_query, att_key, att_value, past_key, past_value):
    rows, wide = att_query.shape
    half = wide // 2
    width = half // CHUNKS
    heads = width // HEAD
    past_rows = past_key.shape[0]
    depth = past_rows * 8 * tps
    far = pl.BlockSpec(memory_space=pltpu.HBM)
    near = pl.BlockSpec(memory_space=pltpu.VMEM)
    dma = pltpu.SemaphoreType.DMA

    def held(*shape):
        return pltpu.VMEM(shape, jnp.bfloat16)

    def wider(*shape):
        return pltpu.VMEM(shape, jnp.float32)

    return pl.pallas_call(
        functools.partial(chain_kernel, tps),
        out_shape=jax.ShapeDtypeStruct((rows, wide), jnp.bfloat16),
        in_specs=[far, far, far, near, near],
        out_specs=far,
        scratch_shapes=[
            held(tps, 2 * past_rows, wide),
            held(tps, 2 * past_rows, wide),
            held(4, 2, tps, 2 * past_rows, half),
            held(CHUNKS, depth, width),
            held(CHUNKS, depth, width),
            held(3, 2, CHUNKS, rows, width),
            held(2, 2, CHUNKS, rows, width),
            held(2, 2, CHUNKS, rows, width),
            held(2, CHUNKS, heads, HEAD, 2 * rows),
            wider(2, CHUNKS, heads, 8, 2 * rows),
            held(2, CHUNKS, heads, HEAD, 2 * rows),
            wider(2, CHUNKS, heads, 8, 2 * rows),
            wider(CHUNKS, heads, HEAD, 2 * rows),
            wider(CHUNKS, heads, 8, 2 * rows),
            held(CHUNKS, 2, rows, width),
            dma((tps,)),
            dma((tps,)),
            dma((1,)),
            dma((2,)),
            dma((4,)),
            dma((4,)),
            dma((3, CHUNKS)),
            dma((3, 2, CHUNKS)),
            dma((2, CHUNKS)),
            dma((2, CHUNKS)),
            dma((2, CHUNKS)),
            dma((2, CHUNKS)),
            dma((2, CHUNKS)),
            dma((2, CHUNKS)),
            dma((2, CHUNKS)),
            dma((CHUNKS,)),
            dma((2, CHUNKS)),
        ],
        compiler_params=pltpu.CompilerParams(
            collective_id=0, has_side_effects=True, vmem_limit_bytes=56 * 2**20
        ),
    )(att_query, att_key, att_value, past_key, past_value)


def local(att_query, att_key, att_value, past_key, past_value):
    seqs, tps = lax.axis_size("seq"), lax.axis_size("tp")
    rows, wide = att_query.shape
    fits = wide % (2 * CHUNKS * HEAD) == 0 and wide * tps == past_key.shape[1]
    if seqs == 8 and fits and past_key.shape[0] == 8 and rows == 128:
        return local_chain(tps, att_query, att_key, att_value, past_key, past_value)
    return local_xla(att_query, att_key, att_value, past_key, past_value)


def solution(mesh):
    placed = (
        P("seq", "tp"),
        P("seq", "tp"),
        P("seq", "tp"),
        P(("seq", "tp"), None),
        P(("seq", "tp"), None),
    )
    return jax.shard_map(
        local, mesh=mesh, in_specs=placed, out_specs=P("seq", "tp"), check_vma=False
    )
```

```python
import functools

import jax
import jax.numpy as jnp
from jax import lax
from jax.experimental import pallas as pl
from jax.experimental.pallas import tpu as pltpu
from jax.sharding import PartitionSpec as P

HEAD = 128


NEGATIVE = -1e30


def split_heads(block):
    return block.reshape(block.shape[0], block.shape[1] // HEAD, HEAD)


def absorb(state, queries, query_pos, keys, values, key_pos):
    maxima, totals, sums = state
    scores = jnp.einsum(
        "hqd,khd->hqk", queries, keys, preferred_element_type=jnp.float32
    ) * HEAD ** (-0.5)
    allowed = key_pos[None, None, :] <= query_pos[None, :, None]
    scores = jnp.where(allowed, scores, NEGATIVE)
    newmax = jnp.maximum(maxima, jnp.max(scores, axis=2))
    factor = jnp.exp(maxima - newmax)
    weights = jnp.where(allowed, jnp.exp(scores - newmax[:, :, None]), 0.0)
    totals = totals * factor + jnp.sum(weights, axis=2)
    sums = sums * factor[:, :, None] + jnp.einsum(
        "hqk,khd->hqd", weights.astype(jnp.bfloat16), values, preferred_element_type=jnp.float32
    )
    return (newmax, totals, sums)


def absorb_when_needed(state, queries, query_pos, keys, values, key_pos):
    return lax.cond(
        jnp.min(key_pos) > jnp.max(query_pos),
        lambda carried: carried,
        lambda carried: absorb(carried, queries, query_pos, keys, values, key_pos),
        state,
    )


def finish(state):
    maxima, totals, sums = state
    result = sums / totals[:, :, None]
    return jnp.transpose(result, (1, 0, 2)).reshape(result.shape[1], -1).astype(jnp.bfloat16)


def empty_state(head_count, count):
    return (
        jnp.full((head_count, count), NEGATIVE, jnp.float32),
        jnp.zeros((head_count, count), jnp.float32),
        jnp.zeros((head_count, count, HEAD), jnp.float32),
    )


def local_xla(att_query, att_key, att_value, past_key, past_value):
    seq_count = lax.axis_size("seq")
    position = lax.axis_index("seq")
    past_keys, past_values = (
        lax.all_to_all(past_key, "tp", split_axis=1, concat_axis=0, tiled=True),
        lax.all_to_all(past_value, "tp", split_axis=1, concat_axis=0, tiled=True),
    )
    past_rows = past_keys.shape[0]
    hist_total = past_rows * seq_count
    rows = att_query.shape[0]
    heads_here = att_query.shape[1] // HEAD
    per_device = max(1, heads_here // seq_count)
    repeat = max(1, seq_count // heads_here)
    span = past_rows + rows

    def spread(block):
        return jnp.tile(split_heads(block), (1, repeat, 1))

    stacked_keys = jnp.concatenate([past_keys, att_key], 0)
    stacked_values = jnp.concatenate([past_values, att_value], 0)
    got_query, got_keys, got_values = (
        lax.all_to_all(spread(att_query), "seq", split_axis=1, concat_axis=0, tiled=True),
        lax.all_to_all(spread(stacked_keys), "seq", split_axis=1, concat_axis=0, tiled=True),
        lax.all_to_all(spread(stacked_values), "seq", split_axis=1, concat_axis=0, tiled=True),
    )
    stretch_total = rows * seq_count
    copy_index = position // heads_here
    piece = stretch_total // (2 * repeat)
    first_start = copy_index * piece
    second_start = (2 * repeat - 1 - copy_index) * piece
    offsets = jnp.arange(piece, dtype=jnp.int32)
    pos_one = hist_total + first_start + offsets
    pos_two = hist_total + second_start + offsets
    query_one = jnp.transpose(lax.dynamic_slice_in_dim(got_query, first_start, piece, 0), (1, 0, 2))
    query_two = jnp.transpose(
        lax.dynamic_slice_in_dim(got_query, second_start, piece, 0), (1, 0, 2)
    )
    source = jnp.arange(seq_count, dtype=jnp.int32)[:, None]
    within = jnp.arange(span, dtype=jnp.int32)[None, :]
    key_table = jnp.where(
        within < past_rows,
        source * past_rows + within,
        hist_total + source * rows + within - past_rows,
    )
    turns = seq_count // 2
    key_blocks = got_keys.reshape(turns, 2 * span, per_device, HEAD)
    value_blocks = got_values.reshape(turns, 2 * span, per_device, HEAD)
    pos_blocks = key_table.reshape(turns, 2 * span)

    def step_block(carry_now, items):
        keys, values, key_pos = items
        return (
            (
                absorb_when_needed(carry_now[0], query_one, pos_one, keys, values, key_pos),
                absorb_when_needed(carry_now[1], query_two, pos_two, keys, values, key_pos),
            ),
            None,
        )

    start_state = empty_state(per_device, piece)
    carry, unused = lax.scan(
        step_block, (start_state, start_state), (key_blocks, value_blocks, pos_blocks)
    )
    placed = jnp.zeros((stretch_total, per_device * HEAD), jnp.bfloat16)
    placed = lax.dynamic_update_slice_in_dim(placed, finish(carry[0]), first_start, 0)
    placed = lax.dynamic_update_slice_in_dim(placed, finish(carry[1]), second_start, 0)
    returned = lax.all_to_all(
        placed.reshape(stretch_total, per_device, HEAD),
        "seq",
        split_axis=0,
        concat_axis=1,
        tiled=True,
    )
    summed = jnp.sum(returned.reshape(rows, repeat, heads_here, HEAD).astype(jnp.float32), axis=1)
    return summed.reshape(rows, heads_here * HEAD).astype(jnp.bfloat16)


SCALE = HEAD ** (-0.5)
LOG2E = 1.4426950408889634
CHUNKS = 4
HEADWAY = 1


def partial(query, pieces, diagonal):
    contract = (((1,), (1,)), ((), ()))
    found = [
        lax.dot_general(query, keys, contract, preferred_element_type=jnp.float32)
        for keys, values in pieces
    ]
    if diagonal:
        shape = found[-1].shape
        query_at = lax.broadcasted_iota(jnp.int32, shape, 0)
        key_at = lax.broadcasted_iota(jnp.int32, shape, 1)
        found[-1] = jnp.where(key_at <= query_at, found[-1], NEGATIVE)
    scores = jnp.concatenate(found, 1)
    highest = jnp.max(scores, axis=1, keepdims=True)
    weights = jnp.exp2((scores - highest) * (SCALE * LOG2E))
    total = jnp.sum(weights, axis=1, keepdims=True)
    rounded = weights.astype(jnp.bfloat16)
    summed = jnp.zeros((query.shape[0], HEAD), jnp.float32)
    start = 0
    for keys, values in pieces:
        stop = start + keys.shape[0]
        summed += jnp.dot(rounded[:, start:stop], values, preferred_element_type=jnp.float32)
        start = stop
    return summed / total, highest * SCALE + jnp.log(total)


def as_row(column):
    return jnp.transpose(jnp.broadcast_to(column, (column.shape[0], HEAD)))[:8]


def as_columns(row):
    return jnp.transpose(jnp.broadcast_to(row, (HEAD, row.shape[1])))


def merge(parts):
    top = functools.reduce(jnp.maximum, [level for rows, level in parts])
    shares = [jnp.exp(level - top) for rows, level in parts]
    every = sum(shares)
    return sum(rows * as_columns(share / every) for (rows, level), share in zip(parts, shares))


def wait(ref, sem):
    pltpu.make_async_copy(ref, ref, sem).wait()


def chain_kernel(
    tps, q_ref, k_ref, v_ref, pk_ref, pv_ref, o_ref,
    hist, hist_tp, slab, past_k, past_v, own, far_q, far_kv, got_o, got_l, give_o, give_l,
    keep_o, keep_l, o_buf,
    tp_send, tp_recv, hy_send, hy_recv, hz_send, hz_recv, own_send, own_recv,
    far_send, far_q_recv, far_kv_recv, go_send, go_recv, gl_send, gl_recv, fin_send, fin_recv,
):
    seqs, zs = 8, 4
    me = lax.axis_index("seq")
    mine = lax.axis_index("tp")
    z, y = me // 2, lax.rem(me, 2)
    peer = z * 2 + 1 - y
    rows, wide = q_ref.shape
    half = wide // 2
    width = half // CHUNKS
    heads = width // HEAD
    mesh_id = pl.DeviceIdType.MESH

    barrier = pltpu.get_barrier_semaphore()
    for off in range(1, seqs):
        pl.semaphore_signal(
            barrier, inc=1, device_id={"seq": lax.rem(me + off, seqs)}, device_id_type=mesh_id
        )
    for off in range(1, tps):
        pl.semaphore_signal(
            barrier, inc=1, device_id={"tp": lax.rem(mine + off, tps)}, device_id_type=mesh_id
        )
    for part in range(tps):
        at = slice(part * wide, (part + 1) * wide)
        both = [pk_ref[:, at].astype(jnp.float32), pv_ref[:, at].astype(jnp.float32)]
        hist[part] = jnp.concatenate(both, 0).astype(jnp.bfloat16)
    pl.semaphore_wait(barrier, seqs + tps - 2)

    def columns(side, chunk):
        return pl.ds(pl.multiple_of(side * half + chunk * width, width), width)

    def send_to(seq, src, dst, send_sem, recv_sem):
        pltpu.make_async_remote_copy(
            src_ref=src, dst_ref=dst, send_sem=send_sem, recv_sem=recv_sem,
            device_id={"seq": seq}, device_id_type=mesh_id,
        ).start()

    for off in range(1, tps):
        other = lax.rem(mine + off, tps)
        pltpu.make_async_remote_copy(
            src_ref=hist.at[other], dst_ref=hist_tp.at[mine],
            send_sem=tp_send.at[off], recv_sem=tp_recv.at[mine],
            device_id={"tp": other}, device_id_type=mesh_id,
        ).start()
    pltpu.make_async_copy(hist.at[mine], hist_tp.at[mine], tp_recv.at[mine]).start()

    def forward(chunk):
        for origin, kind, target, buf, slot, sem in (
            (0, 1, 1, far_kv, 0, far_kv_recv),
            (0, 2, 1, far_kv, 1, far_kv_recv),
            (2, 0, 1, far_q, 0, far_q_recv),
            (3, 0, 1, far_q, 1, far_q_recv),
            (3, 0, 2, far_q, 1, far_q_recv),
        ):
            number = slot if origin == 0 else 2 - target

            @pl.when(z == origin)
            def _():
                send_to(
                    target * 2 + y, own.at[kind, :, chunk], buf.at[slot, :, chunk],
                    far_send.at[number, chunk], sem.at[slot, chunk],
                )

    def send_own(kind, chunk):
        ref = (q_ref, k_ref, v_ref)[kind]
        send_to(
            peer, ref.at[:, columns(1 - y, chunk)], own.at[kind, y, chunk],
            own_send.at[kind, chunk], own_recv.at[kind, y, chunk],
        )
        pltpu.make_async_copy(
            ref.at[:, columns(y, chunk)], own.at[kind, y, chunk], own_recv.at[kind, y, chunk]
        ).start()

    def wait_own(kind, chunk):
        for side in range(2):
            wait(own.at[kind, side, chunk], own_recv.at[kind, side, chunk])

    @pl.when(z >= 2)
    def _():
        for chunk in range(CHUNKS):
            send_own(0, chunk)

    @pl.when(z < 2)
    def _():
        for chunk in range(CHUNKS):
            send_own(1, chunk)
            send_own(2, chunk)

    for part in range(tps):
        wait(hist_tp.at[part], tp_recv.at[part])
    away = hist_tp.at[:, :, pl.ds(pl.multiple_of((1 - y) * half, half), half)]
    here = hist_tp.at[:, :, pl.ds(pl.multiple_of(y * half, half), half)]
    send_to(peer, away, slab.at[z, y], hy_send.at[0], hy_recv.at[y])
    pltpu.make_async_copy(here, slab.at[z, y], hy_recv.at[y]).start()

    @pl.when(z >= 2)
    def _():
        for chunk in range(CHUNKS):
            send_own(1, chunk)
            send_own(2, chunk)
        for chunk in range(HEADWAY):
            wait_own(0, chunk)
            forward(chunk)

    @pl.when(z < 2)
    def _():
        for chunk in range(CHUNKS):
            send_own(0, chunk)

    for side in range(2):
        wait(slab.at[z, side], hy_recv.at[side])

    def pass_slab(number, target):
        send_to(
            target * 2 + y, slab.at[number], slab.at[number], hz_send.at[number], hz_recv.at[number]
        )

    for origin in range(zs):
        pl.when(z == origin)(
            functools.partial(pass_slab, origin, 1 if origin == 0 else origin - 1)
        )

    @pl.when(z == 2)
    def _():
        wait(slab.at[3], hz_recv.at[3])
        pass_slab(3, 1)
        wait(slab.at[2], hz_send.at[2])

    @pl.when(z >= 2)
    def _():
        wait(slab.at[3], hz_send.at[3])

    @pl.when(z >= 2)
    def _():
        for chunk in range(HEADWAY, CHUNKS):
            wait_own(0, chunk)
            forward(chunk)

    @pl.when(z == 0)
    def _():
        for chunk in range(CHUNKS):
            wait_own(1, chunk)
            wait_own(2, chunk)
            forward(chunk)

    def settle(number):
        past_rows = slab.shape[3] // 2
        count = 2 * tps * past_rows
        at = slice(number * count, (number + 1) * count)
        for chunk in range(CHUNKS):
            cut = slice(chunk * width, (chunk + 1) * width)
            blocks = [
                slab[number, side, part, :, cut].astype(jnp.float32)
                for side in range(2)
                for part in range(tps)
            ]
            past_k[chunk, at] = jnp.concatenate([b[:past_rows] for b in blocks], 0).astype(jnp.bfloat16)
            past_v[chunk, at] = jnp.concatenate([b[past_rows:] for b in blocks], 0).astype(jnp.bfloat16)

    def lanes(head):
        return slice(head * HEAD, (head + 1) * HEAD)

    def own_of(kind, chunk, head):
        return own[kind, :, chunk, :, lanes(head)].reshape(2 * rows, HEAD)

    def far_q_of(slot, chunk, head):
        return far_q[slot, :, chunk, :, lanes(head)].reshape(2 * rows, HEAD)

    def near_pair(chunk, head):
        return own_of(1, chunk, head), own_of(2, chunk, head)

    def far_pair(chunk, head):
        return tuple(
            far_kv[kind, :, chunk, :, lanes(head)].reshape(2 * rows, HEAD) for kind in range(2)
        )

    def past_pair(chunk, head, first, last):
        at = slice(first * past_k.shape[1] // zs, last * past_k.shape[1] // zs)
        return past_k[chunk, at, lanes(head)], past_v[chunk, at, lanes(head)]

    def wait_far_q(slot, chunk):
        wait(far_q.at[slot, :, chunk], far_q_recv.at[slot, chunk])

    def give(slot, target, source, chunk):
        send_to(
            target * 2 + y, give_o.at[slot, chunk], got_o.at[source, chunk],
            go_send.at[slot, chunk], go_recv.at[source, chunk],
        )
        send_to(
            target * 2 + y, give_l.at[slot, chunk], got_l.at[source, chunk],
            gl_send.at[slot, chunk], gl_recv.at[source, chunk],
        )

    def put_part(slot, chunk, head, part):
        give_o[slot, chunk, head] = part[0].astype(jnp.bfloat16)
        give_l[slot, chunk, head] = as_row(part[1])

    def put_result(chunk, head, result):
        flat = result.astype(jnp.bfloat16)
        for side in range(2):
            o_buf[chunk, side, :, lanes(head)] = flat[side * rows : (side + 1) * rows]

    def finish_chunk(chunk):
        spot = o_ref.at[:, columns(y, chunk)]
        send_to(peer, o_buf.at[chunk, 1 - y], spot, fin_send.at[chunk], fin_recv.at[y, chunk])
        pltpu.make_async_copy(o_buf.at[chunk, y], spot, fin_recv.at[y, chunk]).start()

    def each_chunk(first, body):
        def step(chunk, unused):
            body(chunk)
            return unused

        lax.fori_loop(first, CHUNKS, step, 0)

    def wait_slabs(numbers):
        for number in numbers:
            wait(slab.at[number], hz_recv.at[number])

    def sent_slabs(numbers):
        for number in numbers:
            wait(slab.at[number], hz_send.at[number])

    def sent_parts(slots):
        def body(chunk):
            for slot in slots:
                wait(give_o.at[slot, chunk], go_send.at[slot, chunk])
                wait(give_l.at[slot, chunk], gl_send.at[slot, chunk])

        each_chunk(0, body)

    @pl.when(z == 0)
    def _():
        wait_slabs((1, 2, 3))
        for number in range(zs):
            settle(number)

        def body(chunk):
            wait_own(0, chunk)
            for head in range(heads):
                pieces = [past_pair(chunk, head, 0, zs), near_pair(chunk, head)]
                put_result(chunk, head, partial(own_of(0, chunk, head), pieces, True)[0])
            finish_chunk(chunk)

        each_chunk(0, body)
        sent_slabs((0,))

    @pl.when(z == 1)
    def _():
        wait_slabs((0,))
        settle(0)
        settle(1)

        def far_part(chunk):
            for kind in range(3):
                wait_own(kind, chunk)
            for kind in range(2):
                wait(far_kv.at[kind, :, chunk], far_kv_recv.at[kind, chunk])
            for slot in (1, 0):
                wait_far_q(slot, chunk)
                for head in range(heads):
                    pieces = [
                        past_pair(chunk, head, 0, 2), far_pair(chunk, head), near_pair(chunk, head)
                    ]
                    put_part(slot, chunk, head, partial(far_q_of(slot, chunk, head), pieces, False))
                give(slot, 2 + slot, 0, chunk)

        def own_part(chunk):
            for head in range(heads):
                pieces = [
                    past_pair(chunk, head, 0, zs), far_pair(chunk, head), near_pair(chunk, head)
                ]
                put_result(chunk, head, partial(own_of(0, chunk, head), pieces, True)[0])
            finish_chunk(chunk)

        def body(chunk):
            far_part(chunk)

            @pl.when(chunk == 0)
            def _():
                for number in (2, 3):
                    wait_slabs((number,))
                    pass_slab(number, 0)
                    settle(number)

            own_part(chunk)

        each_chunk(0, body)
        sent_slabs((1, 2, 3))
        sent_parts((0, 1))

    def keep(chunk, head, part):
        keep_o[chunk, head] = part[0]
        keep_l[chunk, head] = as_row(part[1])

    def combine(sources):
        def body(chunk):
            for source in sources:
                wait(got_o.at[source, chunk], go_recv.at[source, chunk])
                wait(got_l.at[source, chunk], gl_recv.at[source, chunk])
            for head in range(heads):
                parts = [(keep_o[chunk, head], keep_l[chunk, head, :1])]
                for source in sources:
                    parts.append(
                        (
                            got_o[source, chunk, head].astype(jnp.float32),
                            got_l[source, chunk, head, :1],
                        )
                    )
                put_result(chunk, head, merge(parts))
            finish_chunk(chunk)

        each_chunk(0, body)

    @pl.when(z == 2)
    def _():
        settle(2)
        settle(3)

        def body(chunk):
            wait_own(1, chunk)
            wait_own(2, chunk)
            wait_far_q(1, chunk)
            for head in range(heads):
                pieces = [past_pair(chunk, head, 2, zs), near_pair(chunk, head)]
                put_part(1, chunk, head, partial(far_q_of(1, chunk, head), pieces, False))
            give(1, 3, 1, chunk)
            for head in range(heads):
                pieces = [past_pair(chunk, head, 2, zs), near_pair(chunk, head)]
                keep(chunk, head, partial(own_of(0, chunk, head), pieces, True))

        each_chunk(0, body)
        combine((0,))
        sent_parts((1,))

    @pl.when(z == 3)
    def _():
        def body(chunk):
            wait_own(1, chunk)
            wait_own(2, chunk)
            for head in range(heads):
                keep(chunk, head, partial(own_of(0, chunk, head), [near_pair(chunk, head)], True))

        each_chunk(0, body)
        combine((0, 1))

    for off in range(1, tps):
        wait(hist.at[0], tp_send.at[off])
    wait(slab.at[0, 0], hy_send.at[0])

    def last(chunk):
        for kind in range(3):
            wait(own.at[kind, 0, chunk], own_send.at[kind, chunk])
        for origin, targets in ((0, 2), (2, 1), (3, 2)):

            @pl.when(z == origin)
            def _():
                for target in range(targets):
                    wait(far_q.at[0, :, chunk], far_send.at[1 - target if origin == 2 else target, chunk])

        wait(o_buf.at[chunk, 0], fin_send.at[chunk])
        for side in range(2):
            wait(o_ref.at[:, columns(side, chunk)], fin_recv.at[side, chunk])

    each_chunk(0, last)


def local_chain(tps, att_query, att_key, att_value, past_key, past_value):
    rows, wide = att_query.shape
    half = wide // 2
    width = half // CHUNKS
    heads = width // HEAD
    past_rows = past_key.shape[0]
    depth = past_rows * 8 * tps
    far = pl.BlockSpec(memory_space=pltpu.HBM)
    near = pl.BlockSpec(memory_space=pltpu.VMEM)
    dma = pltpu.SemaphoreType.DMA

    def held(*shape):
        return pltpu.VMEM(shape, jnp.bfloat16)

    def wider(*shape):
        return pltpu.VMEM(shape, jnp.float32)

    return pl.pallas_call(
        functools.partial(chain_kernel, tps),
        out_shape=jax.ShapeDtypeStruct((rows, wide), jnp.bfloat16),
        in_specs=[far, far, far, near, near],
        out_specs=far,
        scratch_shapes=[
            held(tps, 2 * past_rows, wide),
            held(tps, 2 * past_rows, wide),
            held(4, 2, tps, 2 * past_rows, half),
            held(CHUNKS, depth, width),
            held(CHUNKS, depth, width),
            held(3, 2, CHUNKS, rows, width),
            held(2, 2, CHUNKS, rows, width),
            held(2, 2, CHUNKS, rows, width),
            held(2, CHUNKS, heads, 2 * rows, HEAD),
            wider(2, CHUNKS, heads, 8, 2 * rows),
            held(2, CHUNKS, heads, 2 * rows, HEAD),
            wider(2, CHUNKS, heads, 8, 2 * rows),
            wider(CHUNKS, heads, 2 * rows, HEAD),
            wider(CHUNKS, heads, 8, 2 * rows),
            held(CHUNKS, 2, rows, width),
            dma((tps,)),
            dma((tps,)),
            dma((1,)),
            dma((2,)),
            dma((4,)),
            dma((4,)),
            dma((3, CHUNKS)),
            dma((3, 2, CHUNKS)),
            dma((2, CHUNKS)),
            dma((2, CHUNKS)),
            dma((2, CHUNKS)),
            dma((2, CHUNKS)),
            dma((2, CHUNKS)),
            dma((2, CHUNKS)),
            dma((2, CHUNKS)),
            dma((CHUNKS,)),
            dma((2, CHUNKS)),
        ],
        compiler_params=pltpu.CompilerParams(
            collective_id=0, has_side_effects=True, vmem_limit_bytes=56 * 2**20
        ),
    )(att_query, att_key, att_value, past_key, past_value)


def local(att_query, att_key, att_value, past_key, past_value):
    seqs, tps = lax.axis_size("seq"), lax.axis_size("tp")
    rows, wide = att_query.shape
    fits = wide % (2 * CHUNKS * HEAD) == 0 and wide * tps == past_key.shape[1]
    if seqs == 8 and fits and past_key.shape[0] == 8 and rows == 128:
        return local_chain(tps, att_query, att_key, att_value, past_key, past_value)
    return local_xla(att_query, att_key, att_value, past_key, past_value)


def solution(mesh):
    placed = (
        P("seq", "tp"),
        P("seq", "tp"),
        P("seq", "tp"),
        P(("seq", "tp"), None),
        P(("seq", "tp"), None),
    )
    return jax.shard_map(
        local, mesh=mesh, in_specs=placed, out_specs=P("seq", "tp"), check_vma=False
    )
```

```python
import functools

import jax
import jax.numpy as jnp
from jax import lax
from jax.experimental import pallas as pl
from jax.experimental.pallas import tpu as pltpu
from jax.sharding import PartitionSpec as P

HEAD = 128
LOG2E = 1.4426950408889634


NEGATIVE = -1e30


def split_heads(block):
    return block.reshape(block.shape[0], block.shape[1] // HEAD, HEAD)


def absorb(state, queries, query_pos, keys, values, key_pos):
    maxima, totals, sums = state
    scores = jnp.einsum(
        "hqd,khd->hqk", queries, keys, preferred_element_type=jnp.float32
    ) * HEAD ** (-0.5)
    allowed = key_pos[None, None, :] <= query_pos[None, :, None]
    scores = jnp.where(allowed, scores, NEGATIVE)
    newmax = jnp.maximum(maxima, jnp.max(scores, axis=2))
    factor = jnp.exp(maxima - newmax)
    weights = jnp.where(allowed, jnp.exp(scores - newmax[:, :, None]), 0.0)
    totals = totals * factor + jnp.sum(weights, axis=2)
    sums = sums * factor[:, :, None] + jnp.einsum(
        "hqk,khd->hqd", weights.astype(jnp.bfloat16), values, preferred_element_type=jnp.float32
    )
    return (newmax, totals, sums)


def absorb_when_needed(state, queries, query_pos, keys, values, key_pos):
    return lax.cond(
        jnp.min(key_pos) > jnp.max(query_pos),
        lambda carried: carried,
        lambda carried: absorb(carried, queries, query_pos, keys, values, key_pos),
        state,
    )


def finish(state):
    maxima, totals, sums = state
    result = sums / totals[:, :, None]
    return jnp.transpose(result, (1, 0, 2)).reshape(result.shape[1], -1).astype(jnp.bfloat16)


def empty_state(head_count, count):
    return (
        jnp.full((head_count, count), NEGATIVE, jnp.float32),
        jnp.zeros((head_count, count), jnp.float32),
        jnp.zeros((head_count, count, HEAD), jnp.float32),
    )


def local_xla(att_query, att_key, att_value, past_key, past_value):
    seq_count = lax.axis_size("seq")
    position = lax.axis_index("seq")
    past_keys, past_values = (
        lax.all_to_all(past_key, "tp", split_axis=1, concat_axis=0, tiled=True),
        lax.all_to_all(past_value, "tp", split_axis=1, concat_axis=0, tiled=True),
    )
    past_rows = past_keys.shape[0]
    hist_total = past_rows * seq_count
    rows = att_query.shape[0]
    heads_here = att_query.shape[1] // HEAD
    per_device = max(1, heads_here // seq_count)
    repeat = max(1, seq_count // heads_here)
    span = past_rows + rows

    def spread(block):
        return jnp.tile(split_heads(block), (1, repeat, 1))

    stacked_keys = jnp.concatenate([past_keys, att_key], 0)
    stacked_values = jnp.concatenate([past_values, att_value], 0)
    got_query, got_keys, got_values = (
        lax.all_to_all(spread(att_query), "seq", split_axis=1, concat_axis=0, tiled=True),
        lax.all_to_all(spread(stacked_keys), "seq", split_axis=1, concat_axis=0, tiled=True),
        lax.all_to_all(spread(stacked_values), "seq", split_axis=1, concat_axis=0, tiled=True),
    )
    stretch_total = rows * seq_count
    copy_index = position // heads_here
    piece = stretch_total // (2 * repeat)
    first_start = copy_index * piece
    second_start = (2 * repeat - 1 - copy_index) * piece
    offsets = jnp.arange(piece, dtype=jnp.int32)
    pos_one = hist_total + first_start + offsets
    pos_two = hist_total + second_start + offsets
    query_one = jnp.transpose(lax.dynamic_slice_in_dim(got_query, first_start, piece, 0), (1, 0, 2))
    query_two = jnp.transpose(
        lax.dynamic_slice_in_dim(got_query, second_start, piece, 0), (1, 0, 2)
    )
    source = jnp.arange(seq_count, dtype=jnp.int32)[:, None]
    within = jnp.arange(span, dtype=jnp.int32)[None, :]
    key_table = jnp.where(
        within < past_rows,
        source * past_rows + within,
        hist_total + source * rows + within - past_rows,
    )
    turns = seq_count // 2
    key_blocks = got_keys.reshape(turns, 2 * span, per_device, HEAD)
    value_blocks = got_values.reshape(turns, 2 * span, per_device, HEAD)
    pos_blocks = key_table.reshape(turns, 2 * span)

    def step_block(carry_now, items):
        keys, values, key_pos = items
        return (
            (
                absorb_when_needed(carry_now[0], query_one, pos_one, keys, values, key_pos),
                absorb_when_needed(carry_now[1], query_two, pos_two, keys, values, key_pos),
            ),
            None,
        )

    start_state = empty_state(per_device, piece)
    carry, unused = lax.scan(
        step_block, (start_state, start_state), (key_blocks, value_blocks, pos_blocks)
    )
    placed = jnp.zeros((stretch_total, per_device * HEAD), jnp.bfloat16)
    placed = lax.dynamic_update_slice_in_dim(placed, finish(carry[0]), first_start, 0)
    placed = lax.dynamic_update_slice_in_dim(placed, finish(carry[1]), second_start, 0)
    returned = lax.all_to_all(
        placed.reshape(stretch_total, per_device, HEAD),
        "seq",
        split_axis=0,
        concat_axis=1,
        tiled=True,
    )
    summed = jnp.sum(returned.reshape(rows, repeat, heads_here, HEAD).astype(jnp.float32), axis=1)
    return summed.reshape(rows, heads_here * HEAD).astype(jnp.bfloat16)


def attend(query, past_keys, past_values, keys, values):
    rows = query.shape[0]
    contract = (((1,), (1,)), ((), ()))
    past = lax.dot_general(query, past_keys, contract, preferred_element_type=jnp.float32)
    here = lax.dot_general(query, keys, contract, preferred_element_type=jnp.float32)
    free = here.shape[1] - rows
    down = lax.broadcasted_iota(jnp.int32, (rows, rows), 0)
    across = lax.broadcasted_iota(jnp.int32, (rows, rows), 1)
    diagonal = jnp.where(across <= down, here[:, free:], NEGATIVE)
    pieces = [past, diagonal] if free == 0 else [past, here[:, :free], diagonal]
    scores = jnp.concatenate(pieces, 1)
    scale = HEAD ** (-0.5)
    highest = jnp.max(scores, axis=1, keepdims=True)
    weights = jnp.exp2((scores - highest) * (scale * LOG2E))
    total = jnp.sum(weights, axis=1, keepdims=True)
    rounded = weights.astype(jnp.bfloat16)
    depth = past_keys.shape[0]
    summed = jnp.dot(rounded[:, :depth], past_values, preferred_element_type=jnp.float32)
    summed += jnp.dot(rounded[:, depth:], values, preferred_element_type=jnp.float32)
    return (summed / total).astype(jnp.bfloat16)


def exchange_kernel(
    seqs, tps, q_ref, k_ref, v_ref, pk_ref, pv_ref, o_ref,
    hist, hist_tp, hist_all, past_k, past_v, q_buf, k_buf, v_buf, o_buf,
    tp_send, tp_recv, hist_send, hist_recv, send, recv, o_send, o_recv,
):
    me = lax.axis_index("seq")
    mine = lax.axis_index("tp")
    rows, wide = q_ref.shape
    width = wide // seqs
    heads = width // HEAD

    barrier = pltpu.get_barrier_semaphore()
    for off in range(1, seqs):
        pl.semaphore_signal(
            barrier, inc=1, device_id={"seq": lax.rem(me + off, seqs)},
            device_id_type=pl.DeviceIdType.MESH,
        )
    for off in range(1, tps):
        pl.semaphore_signal(
            barrier, inc=1, device_id={"tp": lax.rem(mine + off, tps)},
            device_id_type=pl.DeviceIdType.MESH,
        )
    for part in range(tps):
        at = slice(part * wide, (part + 1) * wide)
        both = [pk_ref[:, at].astype(jnp.float32), pv_ref[:, at].astype(jnp.float32)]
        hist[part] = jnp.concatenate(both, 0).astype(jnp.bfloat16)
    pl.semaphore_wait(barrier, seqs + tps - 2)

    def columns(number):
        return pl.ds(pl.multiple_of(number * width, width), width)

    far_first = sorted(range(1, seqs), key=lambda off: abs(off - seqs // 2))
    sent = []
    for off in range(1, tps):
        other = lax.rem(mine + off, tps)
        copy = pltpu.make_async_remote_copy(
            src_ref=hist.at[other], dst_ref=hist_tp.at[mine],
            send_sem=tp_send.at[off], recv_sem=tp_recv.at[mine],
            device_id={"tp": other}, device_id_type=pl.DeviceIdType.MESH,
        )
        copy.start()
        sent.append(copy)
    pltpu.make_async_copy(hist.at[mine], hist_tp.at[mine], tp_recv.at[mine]).start()
    tensors = ((k_ref, k_buf), (q_ref, q_buf), (v_ref, v_buf))
    for number, (ref, buf) in enumerate(tensors):
        for off in far_first:
            other = lax.rem(me + off, seqs)
            copy = pltpu.make_async_remote_copy(
                src_ref=ref.at[:, columns(other)], dst_ref=buf.at[me],
                send_sem=send.at[number, off], recv_sem=recv.at[number, me],
                device_id={"seq": other}, device_id_type=pl.DeviceIdType.MESH,
            )
            copy.start()
            sent.append(copy)
        pltpu.make_async_copy(ref.at[:, columns(me)], buf.at[me], recv.at[number, me]).start()
    for part in range(tps):
        pltpu.make_async_copy(hist_tp.at[part], hist_tp.at[part], tp_recv.at[part]).wait()
    for off in range(1, seqs):
        other = lax.rem(me + off, seqs)
        copy = pltpu.make_async_remote_copy(
            src_ref=hist_tp.at[:, :, columns(other)], dst_ref=hist_all.at[me],
            send_sem=hist_send.at[off], recv_sem=hist_recv.at[me],
            device_id={"seq": other}, device_id_type=pl.DeviceIdType.MESH,
        )
        copy.start()
        sent.append(copy)
    pltpu.make_async_copy(hist_tp.at[:, :, columns(me)], hist_all.at[me], hist_recv.at[me]).start()

    for source in range(seqs):
        pltpu.make_async_copy(hist_all.at[source], hist_all.at[source], hist_recv.at[source]).wait()
        half = hist_all.shape[2] // 2
        blocks = [hist_all[source, part].astype(jnp.float32) for part in range(tps)]
        at = slice(source * tps * half, (source + 1) * tps * half)
        past_k[at, :] = jnp.concatenate([b[:half] for b in blocks], 0).astype(jnp.bfloat16)
        past_v[at, :] = jnp.concatenate([b[half:] for b in blocks], 0).astype(jnp.bfloat16)

    for block in range(seqs):
        for number, (ref, buf) in enumerate(tensors):
            pltpu.make_async_copy(buf.at[block], buf.at[block], recv.at[number, block]).wait()
        count = (block + 1) * rows
        for head in range(heads):
            at = slice(head * HEAD, (head + 1) * HEAD)
            o_buf[block, :, at] = attend(
                q_buf[block, :, at],
                past_k[:, at],
                past_v[:, at],
                k_buf[: block + 1, :, at].reshape(count, HEAD),
                v_buf[: block + 1, :, at].reshape(count, HEAD),
            )

        @pl.when(me != block)
        def _():
            pltpu.make_async_remote_copy(
                src_ref=o_buf.at[block], dst_ref=o_ref.at[:, columns(me)],
                send_sem=o_send.at[block], recv_sem=o_recv.at[me],
                device_id={"seq": block}, device_id_type=pl.DeviceIdType.MESH,
            ).start()

        @pl.when(me == block)
        def _():
            pltpu.make_async_copy(o_buf.at[block], o_ref.at[:, columns(me)], o_recv.at[me]).start()

    for copy in sent:
        copy.wait_send()
    for block in range(seqs):
        spot = o_ref.at[:, block * width : (block + 1) * width]
        pltpu.make_async_copy(spot, spot, o_recv.at[block]).wait()

        @pl.when(me != block)
        def _():
            pltpu.make_async_copy(o_buf.at[block], o_buf.at[block], o_send.at[block]).wait()


def local_kernel(seqs, tps, att_query, att_key, att_value, past_key, past_value):
    rows, wide = att_query.shape
    width = wide // seqs
    past_rows = past_key.shape[0]
    depth = past_rows * seqs * tps
    anywhere = pl.BlockSpec(memory_space=pltpu.HBM)
    near = pl.BlockSpec(memory_space=pltpu.VMEM)
    bf16 = jnp.bfloat16
    dma = pltpu.SemaphoreType.DMA
    return pl.pallas_call(
        functools.partial(exchange_kernel, seqs, tps),
        out_shape=jax.ShapeDtypeStruct((rows, wide), bf16),
        in_specs=[anywhere, anywhere, anywhere, near, near],
        out_specs=anywhere,
        scratch_shapes=[
            pltpu.VMEM((tps, 2 * past_rows, wide), bf16),
            pltpu.VMEM((tps, 2 * past_rows, wide), bf16),
            pltpu.VMEM((seqs, tps, 2 * past_rows, width), bf16),
            pltpu.VMEM((depth, width), bf16),
            pltpu.VMEM((depth, width), bf16),
            pltpu.VMEM((seqs, rows, width), bf16),
            pltpu.VMEM((seqs, rows, width), bf16),
            pltpu.VMEM((seqs, rows, width), bf16),
            pltpu.VMEM((seqs, rows, width), bf16),
            dma((tps,)),
            dma((tps,)),
            dma((seqs,)),
            dma((seqs,)),
            dma((3, seqs)),
            dma((3, seqs)),
            dma((seqs,)),
            dma((seqs,)),
        ],
        compiler_params=pltpu.CompilerParams(
            collective_id=0, has_side_effects=True, vmem_limit_bytes=56 * 2**20
        ),
    )(att_query, att_key, att_value, past_key, past_value)


def local(att_query, att_key, att_value, past_key, past_value):
    seqs, tps = lax.axis_size("seq"), lax.axis_size("tp")
    rows, wide = att_query.shape
    fits = wide % (seqs * HEAD) == 0 and wide * tps == past_key.shape[1]
    if fits and past_key.shape[0] == 8 and rows % 16 == 0 and rows <= 256 and seqs <= 8:
        return local_kernel(seqs, tps, att_query, att_key, att_value, past_key, past_value)
    return local_xla(att_query, att_key, att_value, past_key, past_value)


def solution(mesh):
    placed = (
        P("seq", "tp"),
        P("seq", "tp"),
        P("seq", "tp"),
        P(("seq", "tp"), None),
        P(("seq", "tp"), None),
    )
    return jax.shard_map(
        local, mesh=mesh, in_specs=placed, out_specs=P("seq", "tp"), check_vma=False
    )
```

```python
import functools

import jax
import jax.numpy as jnp
from jax import lax
from jax.experimental import pallas as pl
from jax.experimental.pallas import tpu as pltpu
from jax.sharding import PartitionSpec as P

HEAD = 128
LOG2E = 1.4426950408889634


NEGATIVE = -1e30


def split_heads(block):
    return block.reshape(block.shape[0], block.shape[1] // HEAD, HEAD)


def absorb(state, queries, query_pos, keys, values, key_pos):
    maxima, totals, sums = state
    scores = jnp.einsum(
        "hqd,khd->hqk", queries, keys, preferred_element_type=jnp.float32
    ) * HEAD ** (-0.5)
    allowed = key_pos[None, None, :] <= query_pos[None, :, None]
    scores = jnp.where(allowed, scores, NEGATIVE)
    newmax = jnp.maximum(maxima, jnp.max(scores, axis=2))
    factor = jnp.exp(maxima - newmax)
    weights = jnp.where(allowed, jnp.exp(scores - newmax[:, :, None]), 0.0)
    totals = totals * factor + jnp.sum(weights, axis=2)
    sums = sums * factor[:, :, None] + jnp.einsum(
        "hqk,khd->hqd", weights.astype(jnp.bfloat16), values, preferred_element_type=jnp.float32
    )
    return (newmax, totals, sums)


def absorb_when_needed(state, queries, query_pos, keys, values, key_pos):
    return lax.cond(
        jnp.min(key_pos) > jnp.max(query_pos),
        lambda carried: carried,
        lambda carried: absorb(carried, queries, query_pos, keys, values, key_pos),
        state,
    )


def finish(state):
    maxima, totals, sums = state
    result = sums / totals[:, :, None]
    return jnp.transpose(result, (1, 0, 2)).reshape(result.shape[1], -1).astype(jnp.bfloat16)


def empty_state(head_count, count):
    return (
        jnp.full((head_count, count), NEGATIVE, jnp.float32),
        jnp.zeros((head_count, count), jnp.float32),
        jnp.zeros((head_count, count, HEAD), jnp.float32),
    )


def local_xla(att_query, att_key, att_value, past_key, past_value):
    seq_count = lax.axis_size("seq")
    position = lax.axis_index("seq")
    past_keys, past_values = (
        lax.all_to_all(past_key, "tp", split_axis=1, concat_axis=0, tiled=True),
        lax.all_to_all(past_value, "tp", split_axis=1, concat_axis=0, tiled=True),
    )
    past_rows = past_keys.shape[0]
    hist_total = past_rows * seq_count
    rows = att_query.shape[0]
    heads_here = att_query.shape[1] // HEAD
    per_device = max(1, heads_here // seq_count)
    repeat = max(1, seq_count // heads_here)
    span = past_rows + rows

    def spread(block):
        return jnp.tile(split_heads(block), (1, repeat, 1))

    stacked_keys = jnp.concatenate([past_keys, att_key], 0)
    stacked_values = jnp.concatenate([past_values, att_value], 0)
    got_query, got_keys, got_values = (
        lax.all_to_all(spread(att_query), "seq", split_axis=1, concat_axis=0, tiled=True),
        lax.all_to_all(spread(stacked_keys), "seq", split_axis=1, concat_axis=0, tiled=True),
        lax.all_to_all(spread(stacked_values), "seq", split_axis=1, concat_axis=0, tiled=True),
    )
    stretch_total = rows * seq_count
    copy_index = position // heads_here
    piece = stretch_total // (2 * repeat)
    first_start = copy_index * piece
    second_start = (2 * repeat - 1 - copy_index) * piece
    offsets = jnp.arange(piece, dtype=jnp.int32)
    pos_one = hist_total + first_start + offsets
    pos_two = hist_total + second_start + offsets
    query_one = jnp.transpose(lax.dynamic_slice_in_dim(got_query, first_start, piece, 0), (1, 0, 2))
    query_two = jnp.transpose(
        lax.dynamic_slice_in_dim(got_query, second_start, piece, 0), (1, 0, 2)
    )
    source = jnp.arange(seq_count, dtype=jnp.int32)[:, None]
    within = jnp.arange(span, dtype=jnp.int32)[None, :]
    key_table = jnp.where(
        within < past_rows,
        source * past_rows + within,
        hist_total + source * rows + within - past_rows,
    )
    turns = seq_count // 2
    key_blocks = got_keys.reshape(turns, 2 * span, per_device, HEAD)
    value_blocks = got_values.reshape(turns, 2 * span, per_device, HEAD)
    pos_blocks = key_table.reshape(turns, 2 * span)

    def step_block(carry_now, items):
        keys, values, key_pos = items
        return (
            (
                absorb_when_needed(carry_now[0], query_one, pos_one, keys, values, key_pos),
                absorb_when_needed(carry_now[1], query_two, pos_two, keys, values, key_pos),
            ),
            None,
        )

    start_state = empty_state(per_device, piece)
    carry, unused = lax.scan(
        step_block, (start_state, start_state), (key_blocks, value_blocks, pos_blocks)
    )
    placed = jnp.zeros((stretch_total, per_device * HEAD), jnp.bfloat16)
    placed = lax.dynamic_update_slice_in_dim(placed, finish(carry[0]), first_start, 0)
    placed = lax.dynamic_update_slice_in_dim(placed, finish(carry[1]), second_start, 0)
    returned = lax.all_to_all(
        placed.reshape(stretch_total, per_device, HEAD),
        "seq",
        split_axis=0,
        concat_axis=1,
        tiled=True,
    )
    summed = jnp.sum(returned.reshape(rows, repeat, heads_here, HEAD).astype(jnp.float32), axis=1)
    return summed.reshape(rows, heads_here * HEAD).astype(jnp.bfloat16)


def attend(query, past_keys, past_values, keys, values):
    rows = query.shape[0]
    contract = (((1,), (1,)), ((), ()))
    past = lax.dot_general(query, past_keys, contract, preferred_element_type=jnp.float32)
    here = lax.dot_general(query, keys, contract, preferred_element_type=jnp.float32)
    free = here.shape[1] - rows
    down = lax.broadcasted_iota(jnp.int32, (rows, rows), 0)
    across = lax.broadcasted_iota(jnp.int32, (rows, rows), 1)
    diagonal = jnp.where(across <= down, here[:, free:], NEGATIVE)
    pieces = [past, diagonal] if free == 0 else [past, here[:, :free], diagonal]
    scores = jnp.concatenate(pieces, 1)
    scale = HEAD ** (-0.5)
    highest = jnp.max(scores, axis=1, keepdims=True)
    weights = jnp.exp2((scores - highest) * (scale * LOG2E))
    total = jnp.sum(weights, axis=1, keepdims=True)
    rounded = weights.astype(jnp.bfloat16)
    depth = past_keys.shape[0]
    summed = jnp.dot(rounded[:, :depth], past_values, preferred_element_type=jnp.float32)
    summed += jnp.dot(rounded[:, depth:], values, preferred_element_type=jnp.float32)
    return (summed / total).astype(jnp.bfloat16)


def exchange_kernel(
    seqs, tps, q_ref, k_ref, v_ref, pk_ref, pv_ref, o_ref,
    hist, hist_tp, hist_all, past_k, past_v, q_buf, k_buf, v_buf, o_buf,
    tp_send, tp_recv, hist_send, hist_recv, send, recv, o_send, o_recv,
):
    me = lax.axis_index("seq")
    mine = lax.axis_index("tp")
    rows, wide = q_ref.shape
    width = wide // seqs
    heads = width // HEAD

    barrier = pltpu.get_barrier_semaphore()
    for off in range(1, seqs):
        pl.semaphore_signal(
            barrier, inc=1, device_id={"seq": lax.rem(me + off, seqs)},
            device_id_type=pl.DeviceIdType.MESH,
        )
    for off in range(1, tps):
        pl.semaphore_signal(
            barrier, inc=1, device_id={"tp": lax.rem(mine + off, tps)},
            device_id_type=pl.DeviceIdType.MESH,
        )
    for part in range(tps):
        at = slice(part * wide, (part + 1) * wide)
        both = [pk_ref[:, at].astype(jnp.float32), pv_ref[:, at].astype(jnp.float32)]
        hist[part] = jnp.concatenate(both, 0).astype(jnp.bfloat16)
    pl.semaphore_wait(barrier, seqs + tps - 2)

    def columns(number):
        return pl.ds(pl.multiple_of(number * width, width), width)

    far_first = sorted(range(1, seqs), key=lambda off: abs(off - seqs // 2))
    def lanes(number, head):
        return pl.ds(pl.multiple_of(number * width + head * HEAD, HEAD), HEAD)

    sent = []
    for off in range(1, tps):
        other = lax.rem(mine + off, tps)
        copy = pltpu.make_async_remote_copy(
            src_ref=hist.at[other], dst_ref=hist_tp.at[mine],
            send_sem=tp_send.at[off], recv_sem=tp_recv.at[mine],
            device_id={"tp": other}, device_id_type=pl.DeviceIdType.MESH,
        )
        copy.start()
        sent.append(copy)
    pltpu.make_async_copy(hist.at[mine], hist_tp.at[mine], tp_recv.at[mine]).start()
    tensors = ((k_ref, k_buf), (q_ref, q_buf), (v_ref, v_buf))

    def send_head(head):
        for number, (ref, buf) in enumerate(tensors):
            for off in far_first:
                other = lax.rem(me + off, seqs)
                copy = pltpu.make_async_remote_copy(
                    src_ref=ref.at[:, lanes(other, head)], dst_ref=buf.at[head, me],
                    send_sem=send.at[number, head, off], recv_sem=recv.at[number, head, me],
                    device_id={"seq": other}, device_id_type=pl.DeviceIdType.MESH,
                )
                copy.start()
                sent.append(copy)
            pltpu.make_async_copy(
                ref.at[:, lanes(me, head)], buf.at[head, me], recv.at[number, head, me]
            ).start()

    send_head(0)
    for part in range(tps):
        pltpu.make_async_copy(hist_tp.at[part], hist_tp.at[part], tp_recv.at[part]).wait()
    for off in range(1, seqs):
        other = lax.rem(me + off, seqs)
        copy = pltpu.make_async_remote_copy(
            src_ref=hist_tp.at[:, :, columns(other)], dst_ref=hist_all.at[me],
            send_sem=hist_send.at[off], recv_sem=hist_recv.at[me],
            device_id={"seq": other}, device_id_type=pl.DeviceIdType.MESH,
        )
        copy.start()
        sent.append(copy)
    pltpu.make_async_copy(hist_tp.at[:, :, columns(me)], hist_all.at[me], hist_recv.at[me]).start()

    for head in range(1, heads):
        send_head(head)

    for source in range(seqs):
        pltpu.make_async_copy(hist_all.at[source], hist_all.at[source], hist_recv.at[source]).wait()
        half = hist_all.shape[2] // 2
        blocks = [hist_all[source, part].astype(jnp.float32) for part in range(tps)]
        at = slice(source * tps * half, (source + 1) * tps * half)
        past_k[at, :] = jnp.concatenate([b[:half] for b in blocks], 0).astype(jnp.bfloat16)
        past_v[at, :] = jnp.concatenate([b[half:] for b in blocks], 0).astype(jnp.bfloat16)

    for head in range(heads):
        at = slice(head * HEAD, (head + 1) * HEAD)
        for block in range(seqs):
            for number, (ref, buf) in enumerate(tensors):
                spot = buf.at[head, block]
                pltpu.make_async_copy(spot, spot, recv.at[number, head, block]).wait()
            count = (block + 1) * rows
            o_buf[head, block] = attend(
                q_buf[head, block],
                past_k[:, at],
                past_v[:, at],
                k_buf[head, : block + 1].reshape(count, HEAD),
                v_buf[head, : block + 1].reshape(count, HEAD),
            )

            @pl.when(me != block)
            def _():
                pltpu.make_async_remote_copy(
                    src_ref=o_buf.at[head, block], dst_ref=o_ref.at[:, lanes(me, head)],
                    send_sem=o_send.at[head, block], recv_sem=o_recv.at[head, me],
                    device_id={"seq": block}, device_id_type=pl.DeviceIdType.MESH,
                ).start()

            @pl.when(me == block)
            def _():
                pltpu.make_async_copy(
                    o_buf.at[head, block], o_ref.at[:, lanes(me, head)], o_recv.at[head, me]
                ).start()

    for copy in sent:
        copy.wait_send()
    for head in range(heads):
        for block in range(seqs):
            spot = o_ref.at[:, lanes(block, head)]
            pltpu.make_async_copy(spot, spot, o_recv.at[head, block]).wait()

            @pl.when(me != block)
            def _():
                spot = o_buf.at[head, block]
                pltpu.make_async_copy(spot, spot, o_send.at[head, block]).wait()


def local_kernel(seqs, tps, att_query, att_key, att_value, past_key, past_value):
    rows, wide = att_query.shape
    width = wide // seqs
    past_rows = past_key.shape[0]
    depth = past_rows * seqs * tps
    anywhere = pl.BlockSpec(memory_space=pltpu.HBM)
    near = pl.BlockSpec(memory_space=pltpu.VMEM)
    bf16 = jnp.bfloat16
    dma = pltpu.SemaphoreType.DMA
    return pl.pallas_call(
        functools.partial(exchange_kernel, seqs, tps),
        out_shape=jax.ShapeDtypeStruct((rows, wide), bf16),
        in_specs=[anywhere, anywhere, anywhere, near, near],
        out_specs=anywhere,
        scratch_shapes=[
            pltpu.VMEM((tps, 2 * past_rows, wide), bf16),
            pltpu.VMEM((tps, 2 * past_rows, wide), bf16),
            pltpu.VMEM((seqs, tps, 2 * past_rows, width), bf16),
            pltpu.VMEM((depth, width), bf16),
            pltpu.VMEM((depth, width), bf16),
            pltpu.VMEM((width // HEAD, seqs, rows, HEAD), bf16),
            pltpu.VMEM((width // HEAD, seqs, rows, HEAD), bf16),
            pltpu.VMEM((width // HEAD, seqs, rows, HEAD), bf16),
            pltpu.VMEM((width // HEAD, seqs, rows, HEAD), bf16),
            dma((tps,)),
            dma((tps,)),
            dma((seqs,)),
            dma((seqs,)),
            dma((3, width // HEAD, seqs)),
            dma((3, width // HEAD, seqs)),
            dma((width // HEAD, seqs)),
            dma((width // HEAD, seqs)),
        ],
        compiler_params=pltpu.CompilerParams(
            collective_id=0, has_side_effects=True, vmem_limit_bytes=56 * 2**20
        ),
    )(att_query, att_key, att_value, past_key, past_value)


def local(att_query, att_key, att_value, past_key, past_value):
    seqs, tps = lax.axis_size("seq"), lax.axis_size("tp")
    rows, wide = att_query.shape
    fits = wide % (seqs * HEAD) == 0 and wide * tps == past_key.shape[1]
    if fits and past_key.shape[0] == 8 and rows % 16 == 0 and rows <= 256 and seqs <= 8:
        return local_kernel(seqs, tps, att_query, att_key, att_value, past_key, past_value)
    return local_xla(att_query, att_key, att_value, past_key, past_value)


def solution(mesh):
    placed = (
        P("seq", "tp"),
        P("seq", "tp"),
        P("seq", "tp"),
        P(("seq", "tp"), None),
        P(("seq", "tp"), None),
    )
    return jax.shard_map(
        local, mesh=mesh, in_specs=placed, out_specs=P("seq", "tp"), check_vma=False
    )
```
